128 devices in a mesh: inst: 8 (over x, y_lo), span: 16 (over z, y_hi, core).
Axes of the slice: x: 4, y: 4 (y_hi: 2, y_lo: 2; y = y_hi * 2 + y_lo), z: 4, core: 2. Of those that a mesh axis runs over, the one named last changes fastest.
Arguments:
- adjoint_start: float32 [32, 4, 49152], P('inst', None, 'span'), may hold values from -6 to 6
- source: float32 [32, 4, 49152], P('inst', None, 'span'), may hold values from -6 to 6
- jacobian_tiles: bfloat16 [32, 192, 3, 256, 256], P('inst', 'span'), may hold values from -0.21875 to 0.21875
- tile_columns: int32 [192, 3], P('span'), may hold values from -1 to 12
- pseudo_time: float32 [49152], P('span'), may hold values from 0.5 to 4
- control_terms: float32 [3, 32, 49152], P(None, 'inst', 'span'), may hold values from -4 to 4
- surface_rows: int32 [12288], P('span'), may hold values from 0 to 3071
- surface_weight: float32 [3, 12288], replicated, may hold values from -0.009765625 to 0.009765625
- trim_inverse: float32 [3, 3], replicated, may hold values from -4 to 4
Outputs:
- adjoint: float32 [32, 4, 49152], P('inst', None, 'span')
- residual: float32 [32, 4, 49152], P('inst', None, 'span')
The draws below stay inside these ranges and needn't reach their ends.
Inputs may be any that keep to these rules, and one draw needn't show every extreme that they name: `tile_columns`: -1 names the last block row of the span block before, 12 the first of the next. `surface_rows`: a row of the entry's own span block.
All inputs are finite; a program needn't handle non-finite values.
Results may differ from the reference program's by a relative error of at most 0.0016.
Values may be sent and summed in bfloat16 or wider, within the bound.
A program may use at most 128 MiB of HBM per device.

```python
import math
import jax
import jax.numpy as jnp
from jax import lax

INSTANCES = 32
NOBJ = 4
NTRIM = 3
TILE = 256
K = 3
NB = 12
SWEEPS = 2
ROWS = 3072
NBLK = 192
ROWS_ALL = 49152
S_DEV = 768
SURF = 12288


def touch_ends(entries, stream_key, least, high):
    longest = entries.shape.index(max(entries.shape))
    spots = []
    for shift in (0, 1):
        where = [jax.random.randint(jax.random.fold_in(stream_key, axis), (), 0, length) for axis, length in enumerate(entries.shape)]
        where[longest] = (where[longest] + shift) % entries.shape[longest]
        spots.append(tuple(where))
    return entries.at[spots[0]].set(least).at[spots[1]].set(high)


def levels(own_key, extent, pieces, low, top_value):
    gain, own = 1.0, jax.random.fold_in(own_key, 6)
    for position, shards_of in pieces:
        steps = jnp.exp(jax.random.uniform(jax.random.fold_in(own, position), (shards_of,), jnp.float32, low / len(pieces), top_value / len(pieces)))
        gain = gain * jnp.repeat(steps, extent[position] // shards_of).reshape([-1 if axis == position else 1 for axis in range(len(extent))])
    return gain


def normal_values(rng, dims, scale, bound, cuts=(), kind=jnp.bfloat16):
    factor_of = levels(rng, dims, cuts, -0.22, 0.18) if cuts else 1.0
    values = jax.random.normal(rng, dims, jnp.float32) * scale * factor_of
    return jnp.minimum(jnp.maximum(values, -bound), bound).astype(kind)


def setup_inputs(seed: int = 0) -> dict:
    key_of = jax.random.split(jax.random.key(seed), 10)
    adjoint_start = normal_values(key_of[0], (INSTANCES, NOBJ, ROWS_ALL), 1.0, 6.0, ((0, 8), (2, 16)), jnp.float32)
    source = normal_values(key_of[1], (INSTANCES, NOBJ, ROWS_ALL), 1.0, 6.0, ((0, 8), (2, 16)), jnp.float32)
    jacobian_tiles = normal_values(key_of[2], (INSTANCES, NBLK, K, TILE, TILE), (K * TILE) ** -0.5, 0.21875, ((0, 8), (1, 16)))
    tile_columns = touch_ends(jax.random.randint(key_of[3], (NBLK, K), -1, NB + 1), jax.random.fold_in(key_of[3], 1), -1, NB).astype(jnp.int32)
    pseudo_time = jnp.clip(jnp.exp(math.log(4.0) - 2.0794415 * jax.random.uniform(key_of[4], (ROWS_ALL,), jnp.float32) ** levels(key_of[4], (ROWS_ALL,), ((0, 16),), -0.2, 0.2)), 0.5, 4.0)
    control_terms = normal_values(key_of[5], (NTRIM, INSTANCES, ROWS_ALL), 0.5, 4.0, ((1, 8), (2, 16)), jnp.float32)
    surface_rows = touch_ends(jax.random.randint(key_of[6], (SURF,), 0, ROWS), jax.random.fold_in(key_of[6], 1), 0, ROWS - 1).astype(jnp.int32)
    surface_weight = normal_values(key_of[7], (NTRIM, SURF), (INSTANCES * SURF) ** -0.5, 0.009765625, (), jnp.float32)
    trim_inverse = normal_values(key_of[8], (NTRIM, NTRIM), 1.0, 4.0, (), jnp.float32)
    return dict(adjoint_start=adjoint_start, source=source, jacobian_tiles=jacobian_tiles, tile_columns=tile_columns, pseudo_time=pseudo_time, control_terms=control_terms, surface_rows=surface_rows, surface_weight=surface_weight, trim_inverse=trim_inverse)


rotor_rate = 0.25
relaxation = 0.8
highest = lax.Precision.HIGHEST


def tables(period):
    angles = 2.0 * math.pi * jnp.arange(period, dtype=jnp.float32) / period
    half = period // 2
    frequency = jnp.arange(half + 1, dtype=jnp.float32)
    cosine = jnp.cos(frequency[:, None] * angles[None, :])
    sine_table = jnp.sin(frequency[:, None] * angles[None, :])
    spread = angles[:, None] - angles[None, :]
    orders = jnp.arange(1, half, dtype=jnp.float32)
    deriv = -(2.0 / period) * jnp.sum(orders[:, None, None] * jnp.sin(orders[:, None, None] * spread[None]), axis=0)
    weights = jnp.where((frequency == 0) | (frequency == half), 1.0 / period, 2.0 / period).astype(jnp.float32)
    return angles, frequency, cosine, sine_table, deriv, weights


def reference(adjoint_start, source, jacobian_tiles, tile_columns, pseudo_time, control_terms, surface_rows, surface_weight, trim_inverse):
    angles, frequency, cosine, sine_table, deriv, weights = tables(INSTANCES)
    harmonics = jnp.stack([jnp.ones_like(angles), jnp.cos(angles), jnp.sin(angles)])
    block_ids = jnp.arange(NBLK, dtype=jnp.int32)
    targets = ((block_ids // NB) * NB)[:, None] + tile_columns
    valid = ((targets >= 0) & (targets < NBLK)).astype(jnp.float32)
    clipped = jnp.clip(targets, 0, NBLK - 1).astype(jnp.int32)
    surface_index = ((jnp.arange(SURF, dtype=jnp.int32) // S_DEV) * ROWS + surface_rows).astype(jnp.int32)
    scaling = weights[:, None] / (pseudo_time[None, :] + rotor_rate * frequency[:, None])

    def one_instance(pair_items):
        state_row, tiles = pair_items
        narrow = lax.optimization_barrier(state_row.astype(jnp.bfloat16))
        blocks = narrow.astype(jnp.float32).reshape(NOBJ, NBLK, TILE)
        picked = blocks[:, clipped, :] * valid[None, :, :, None]
        result = jnp.einsum('obkr,bkrs->obs', picked, tiles.astype(jnp.float32), precision=highest)
        return result.reshape(NOBJ, NBLK * TILE)

    state_now = adjoint_start
    residual = adjoint_start
    for sweep_idx in range(SWEEPS):
        product = lax.map(one_instance, (state_now, jacobian_tiles))
        surface = state_now[:, :, surface_index]
        weighted = jnp.einsum('ci,ios->cos', harmonics, surface, precision=highest)
        load_sums = jnp.sum(weighted * surface_weight[:, None, :], axis=2)
        multiplier = jnp.dot(trim_inverse, load_sums, precision=highest)
        control = jnp.einsum('cir,co->ior', control_terms, multiplier, precision=highest)
        base_term = source - product - control
        residual = base_term + rotor_rate * jnp.einsum('nm,mor->nor', deriv, state_now, precision=highest)
        cos_sum = jnp.einsum('fm,mor->for', cosine, residual, precision=highest)
        sin_sum = jnp.einsum('fm,mor->for', sine_table, residual, precision=highest)
        update = jnp.einsum('fn,for->nor', cosine, cos_sum * scaling[:, None, :], precision=highest)
        update = update + jnp.einsum('fn,for->nor', sine_table, sin_sum * scaling[:, None, :], precision=highest)
        state_now = state_now + relaxation * update
    return state_now, residual
```

```python
import math

import jax
import jax.numpy as jnp
import ml_dtypes
import numpy as np
from jax import lax
from jax.experimental import pallas as pl
from jax.experimental.pallas import tpu as pltpu
from jax.sharding import PartitionSpec as P

MESH = pl.DeviceIdType.MESH
F32 = jnp.float32
BF16 = jnp.bfloat16

INST = 32
PEERS = 8
OWN = 4
NOBJ = 4
ROWS = 3072
NB = 12
K = 3
TILE = 256
S_DEV = 768
RATE = 0.25
RELAX = 0.8


def split_const(a):
    hi = a.astype(ml_dtypes.bfloat16)
    lo = (a - hi.astype(np.float64)).astype(ml_dtypes.bfloat16)
    return np.concatenate([hi, hi, lo], axis=-1)


def constants():
    theta = 2.0 * math.pi * np.arange(INST) / INST
    half = INST // 2
    trans = np.concatenate(
        [
            np.cos(np.arange(half + 1)[:, None] * theta[None, :]),
            np.sin(np.arange(1, half)[:, None] * theta[None, :]),
        ]
    )
    spread = theta[:, None] - theta[None, :]
    orders = np.arange(1, half)[:, None, None]
    deriv = -(2.0 / INST) * np.sum(orders * np.sin(orders * spread[None]), axis=0)
    eye = np.eye(NOBJ)
    forward = np.kron(trans, eye)
    back = np.kron(trans.T, eye)
    forward_deriv = RATE * np.kron(trans @ deriv, eye)
    own_deriv = RATE * np.kron(deriv, eye)
    mats = np.stack([split_const(m) for m in (forward, back, forward_deriv, own_deriv)])
    angle = np.repeat(theta, NOBJ)
    harm = np.stack([np.cos(angle), np.sin(angle)]).astype(np.float32)
    harm = np.ascontiguousarray(np.broadcast_to(harm[:, :, None], (2, 128, 128)))
    return mats, harm


def exact_dot(mat, x):
    hi = x.astype(BF16)
    lo = (x - hi.astype(F32)).astype(BF16)
    return jnp.dot(mat, jnp.concatenate([hi, lo, hi], axis=0), preferred_element_type=F32)


def kernel(
    n_span,
    cols_ref,
    tinv_ref,
    state_hbm,
    source_hbm,
    jac_hbm,
    pt_hbm,
    ct_hbm,
    rows_hbm,
    sw_hbm,
    mats_hbm,
    harm_hbm,
    adj_hbm,
    res_hbm,
    jbuf,
    st_v,
    src_v,
    ct_v,
    pt_v,
    rows_v,
    sw_v,
    mats_v,
    harm_v,
    out_a,
    out_r,
    s0,
    n0,
    n1,
    nf,
    w_v,
    base1,
    base2,
    xs,
    xb1,
    xb2,
    scal,
    yd,
    ns,
    ds_,
    dr,
    as_,
    ar,
    r1s,
    r1r,
    r2s,
    r2r,
    j_sem,
    l_sem,
    st_send,
    st_recv,
    h0_send,
    h0_recv,
    b_send,
    b_recv,
    n_send,
    n_recv,
    h1_send,
    h1_recv,
    d_send,
    d_recv,
    a_send,
    a_recv,
    r1_send,
    r1_recv,
    r2_send,
    r2_recv,
):
    me = lax.axis_index("inst")
    sp = lax.axis_index("span")
    last = n_span - 1

    local_in = [
        (state_hbm, st_v),
        (rows_hbm, rows_v),
        (sw_hbm.at[:, pl.ds(pl.multiple_of(sp * S_DEV, S_DEV), S_DEV)], sw_v),
        (harm_hbm, harm_v),
        (source_hbm, src_v),
        (ct_hbm, ct_v),
        (pt_hbm, pt_v),
        (mats_hbm, mats_v),
    ]
    loads = [pltpu.make_async_copy(a, b, l_sem.at[n]) for n, (a, b) in enumerate(local_in)]
    for c in loads:
        c.start()

    def jac_copy(b):
        return pltpu.make_async_copy(jac_hbm.at[:, b], jbuf.at[b], j_sem.at[b])

    @pl.loop(0, NB)
    def _(b):
        jac_copy(b).start()

    zero2 = jnp.zeros((2, 16, 128), BF16)
    n1[0, 6:8] = zero2
    n1[4, 0:2] = zero2
    for column in (0, NB + 1):
        n0[column] = jnp.zeros((16, TILE), BF16)

    barrier = pltpu.get_barrier_semaphore()

    def signal(i, s):
        pl.semaphore_signal(barrier, inc=1, device_id=(i, s), device_id_type=MESH)

    def peers(fn):
        @pl.loop(1, PEERS)
        def _(d):
            fn(lax.rem(me + d, PEERS))

    def spans(fn):
        @pl.loop(1, n_span)
        def _(d):
            fn(lax.rem(sp + d, n_span))

    peers(lambda p: signal(p, sp))
    spans(lambda q: signal(me, q))

    has_low = sp > 0
    has_high = sp < last
    def at_low(fn):
        @pl.when(has_low)
        def _():
            @pl.when(me < 2)
            def _():
                pl.loop(0, PEERS)(fn)

    def at_high(fn):
        @pl.when(has_high)
        def _():
            @pl.when(me >= PEERS - 2)
            def _():
                pl.loop(0, PEERS)(fn)

    def around(p):
        signal(p, lax.rem(sp + 1, n_span))
        signal(p, lax.rem(sp + n_span - 1, n_span))

    peers(around)

    loads[0].wait()
    flat = jnp.concatenate([st_v[i] for i in range(OWN)], axis=0)
    for q in range(24):
        piece = flat[:, q * 128 : (q + 1) * 128]
        s0[q // 8, q % 8] = piece
    for b in range(NB):
        n0[b + 1] = flat[:, b * TILE : (b + 1) * TILE].astype(BF16)

    pl.semaphore_wait(barrier, 3 * (PEERS - 1) + n_span - 1)

    def to(src, dst, send, recv, i, s):
        return pltpu.make_async_remote_copy(
            src_ref=src, dst_ref=dst, send_sem=send, recv_sem=recv, device_id=(i, s), device_id_type=MESH
        )

    def halo0_low():
        return to(n0.at[1], n0.at[NB + 1], h0_send.at[0], h0_recv.at[0], me, sp - 1)

    def halo0_high():
        return to(n0.at[NB], n0.at[0], h0_send.at[1], h0_recv.at[1], me, sp + 1)

    def state_out(p):
        return to(s0.at[:, p], xs.at[me], st_send.at[p], st_recv.at[me], p, sp)

    def base_out(k, t, p):
        src, dst = (base1, xb1) if k == 0 else (base2, xb2)
        return to(src.at[t, p], dst.at[me, t], b_send.at[k, t, p], b_recv.at[k, t, me], p, sp)

    def narrow_out(p):
        return to(ns.at[p], n1.at[pl.ds(1, 3), me], n_send.at[p], n_recv.at[me], p, sp)

    def halo1_low(p):
        return to(ns.at[p, 0], n1.at[4, me], h1_send.at[0, p], h1_recv.at[me], p, sp - 1)

    def halo1_high(p):
        return to(ns.at[p, 2], n1.at[0, me], h1_send.at[1, p], h1_recv.at[me], p, sp + 1)

    def deriv_out(p):
        return to(ds_.at[p], dr.at[:, me], d_send.at[p], d_recv.at[me], p, sp)

    def adj_out(p):
        return to(as_.at[p], ar.at[:, me], a_send.at[p], a_recv.at[me], p, sp)

    def sum1_out(k, q):
        return to(r1s.at[k], r1r.at[k, sp], r1_send.at[k, q], r1_recv.at[k, sp], me, q)

    def sum2_out(k, p):
        return to(r2s.at[k], r2r.at[k, me], r2_send.at[k, p], r2_recv.at[k, me], p, sp)

    def arrived(dst, sem):
        pltpu.make_async_copy(dst, dst, sem).wait()

    @pl.when(has_low)
    def _():
        halo0_low().start()

    @pl.when(has_high)
    def _():
        halo0_high().start()

    loads[1].wait()
    loads[2].wait()
    rows = jnp.concatenate([rows_v[q : q + 1, :] for q in range(6)], axis=1)
    high, low = lax.div(rows, 128), lax.rem(rows, 128)
    tiles24 = lax.broadcasted_iota(jnp.int32, (24, S_DEV), 0)
    hit = jnp.broadcast_to(high, (24, S_DEV)) == tiles24
    spread = jnp.concatenate(
        [jnp.where(hit, jnp.broadcast_to(sw_v[c : c + 1, :], (24, S_DEV)), 0.0) for c in range(3)], axis=0
    )
    spread_hi = spread.astype(BF16)
    spread_lo = (spread - spread_hi.astype(F32)).astype(BF16)
    lane_hit = jnp.broadcast_to(low, (128, S_DEV)) == lax.broadcasted_iota(jnp.int32, (128, S_DEV), 0)
    lane_hit = jnp.where(lane_hit, 1.0, 0.0).astype(BF16)
    nt = (((1,), (1,)), ((), ()))
    w_v[...] = lax.dot_general(spread_hi, lane_hit, nt, preferred_element_type=F32) + lax.dot_general(
        spread_lo, lane_hit, nt, preferred_element_type=F32
    )

    lane8 = lax.broadcasted_iota(jnp.int32, (8, 128), 1)
    row8 = lax.rem(lax.broadcasted_iota(jnp.int32, (8, 128), 0), NOBJ)

    def load_row(accs):
        total = jnp.zeros((8, 128), F32)
        for c in range(3):
            col = jnp.sum(accs[c], axis=1, keepdims=True)
            total = total + jnp.where(lane8 == c * NOBJ + row8, jnp.broadcast_to(col, (8, 128)), 0.0)
        return jnp.sum(total, axis=0, keepdims=True)

    loads[3].wait()
    accs = []
    for c in range(3):
        acc = jnp.zeros((16, 128), F32)
        for q in range(24):
            acc = acc + s0[q // 8, q % 8] * jnp.broadcast_to(w_v[c * 24 + q : c * 24 + q + 1, :], (16, 128))
        if c > 0:
            acc = acc * harm_v[c - 1, pl.ds(pl.multiple_of(me * 16, 16), 16), :]
        accs.append(acc[0:8] + acc[8:16])

    def start_sum(k, row):
        r1s[k] = row
        r1r[k, pl.ds(sp, 1)] = row.reshape(1, 1, 128)
        spans(lambda q: sum1_out(k, q).start())

    start_sum(0, load_row(accs))
    peers(lambda p: state_out(p).start())
    xs[pl.ds(me, 1)] = s0[:, pl.ds(me, 1)].reshape(1, 3, 16, 128)

    def middle_sum(k):
        spans(lambda q: arrived(r1r.at[k, q], r1_recv.at[k, q]))
        row = jnp.sum(r1r[k], axis=0)
        r2s[k] = row
        r2r[k, pl.ds(me, 1)] = row.reshape(1, 1, 128)
        peers(lambda p: sum2_out(k, p).start())

    lane16 = lax.broadcasted_iota(jnp.int32, (16, 128), 1)
    row16 = lax.rem(lax.broadcasted_iota(jnp.int32, (16, 128), 0), NOBJ)

    def multiplier(k):
        peers(lambda p: arrived(r2r.at[k, p], r2_recv.at[k, p]))
        row = jnp.broadcast_to(jnp.sum(r2r[k], axis=0), (16, 128))
        out = []
        for c in range(3):
            mask = jnp.zeros((16, 128), F32)
            for d in range(3):
                mask = jnp.where(lane16 == d * NOBJ + row16, tinv_ref[c, d], mask)
            col = jnp.sum(row * mask, axis=1, keepdims=True)
            out.append(jnp.broadcast_to(col, (16, 128)))
        return out

    inst_row = lax.div(lax.broadcasted_iota(jnp.int32, (16, TILE), 0), NOBJ)
    masks = [jnp.where(inst_row == i, 1.0, 0.0).astype(BF16) for i in range(OWN)]

    def product(b, narrow, base):
        acc = jnp.zeros((16, TILE), F32)
        for k in range(K):
            block = narrow[cols_ref[b, k] + 1]
            for i in range(OWN):
                acc = acc + jnp.dot(block * masks[i], jbuf[b, i, k], preferred_element_type=F32)
        for half in range(2):
            q = 2 * b + half
            base[lax.div(q, 8), lax.rem(q, 8)] = acc[:, half * 128 : (half + 1) * 128]

    row8i = lax.div(lax.broadcasted_iota(jnp.int32, (8, 128), 0), NOBJ)

    def finish(q, k, base, mult):
        lanes = pl.ds(pl.multiple_of(q * 128, 128), 128)
        t, p = lax.div(q, 8), lax.rem(q, 8)
        value = jnp.concatenate([src_v[i, :, lanes] for i in range(OWN)], axis=0) - base[t, p]
        for c in range(3):
            parts = []
            for h in range(2):
                first = jnp.broadcast_to(ct_v[c, 2 * h : 2 * h + 1, lanes], (8, 128))
                second = jnp.broadcast_to(ct_v[c, 2 * h + 1 : 2 * h + 2, lanes], (8, 128))
                parts.append(jnp.where(row8i == 0, first, second))
            value = value - jnp.concatenate(parts, axis=0) * mult[c]
        base[t, p] = value

        @pl.when(p != me)
        def _():
            base_out(k, t, p).start()

        @pl.when(p == me)
        def _():
            (xb1 if k == 0 else xb2)[me, t] = value

    def sweep_products(k, narrow, base, between):
        def one(b):
            if k == 0:
                jac_copy(b).wait()
            product(b, narrow, base)

        pl.loop(0, 4)(one)
        middle_sum(k)
        pl.loop(4, 8)(one)
        between()
        mult = multiplier(k)
        pl.loop(0, 16)(lambda q: finish(q, k, base, mult))

        @pl.loop(8, NB)
        def _(b):
            one(b)
            finish(2 * b, k, base, mult)
            finish(2 * b + 1, k, base, mult)

    def wide(ref):
        return jnp.concatenate([ref[:, t].reshape(128, 128) for t in range(3)], axis=1)

    @pl.when(has_high)
    def _():
        arrived(n0.at[NB + 1], h0_recv.at[0])

    @pl.when(has_low)
    def _():
        arrived(n0.at[0], h0_recv.at[1])

    def first_between():
        for c in loads[4:]:
            c.wait()
        order = lax.div(lax.broadcasted_iota(jnp.int32, (128, 128), 0), NOBJ)
        freq = jnp.where(order > INST // 2, order - INST // 2, order)
        ends = jnp.logical_or(freq == 0, freq == INST // 2)
        weight = jnp.where(ends, RELAX / INST, 2.0 * RELAX / INST)
        offset = RATE * freq.astype(F32)
        for t in range(3):
            pt = jnp.broadcast_to(pt_v[t, pl.ds(me, 1), :], (128, 128))
            scal[:, t * 128 : (t + 1) * 128] = weight / (pt + offset)
        peers(lambda p: arrived(xs.at[p], st_recv.at[p]))
        yd[...] = exact_dot(mats_v[2], wide(xs))

    sweep_products(0, n0, base1, first_between)

    def wait_base(k):
        @pl.loop(0, 3)
        def _(t):
            peers(lambda p: arrived((xb1 if k == 0 else xb2).at[p, t], b_recv.at[k, t, p]))

    wait_base(0)
    spectrum = exact_dot(mats_v[0], wide(xb1)) + yd[...]
    state1 = wide(xs) + exact_dot(mats_v[1], spectrum * scal[...])
    for t in range(3):
        piece = state1[:, t * 128 : (t + 1) * 128]
        xs[:, t] = piece.reshape(PEERS, 16, 128)
        ns[:, t] = piece.astype(BF16).reshape(PEERS, 16, 128)
    peers(lambda p: narrow_out(p).start())

    at_low(lambda p: halo1_low(p).start())
    at_high(lambda p: halo1_high(p).start())

    n1[pl.ds(1, 3), pl.ds(me, 1)] = ns[pl.ds(me, 1)].reshape(3, 1, 16, 128)

    accs = []
    for c in range(3):
        acc = jnp.zeros((128, 128), F32)
        for t in range(3):
            weight = w_v[pl.ds(c * 24 + t * 8 + me, 1), :]
            acc = acc + state1[:, t * 128 : (t + 1) * 128] * jnp.broadcast_to(weight, (128, 128))
        if c > 0:
            acc = acc * harm_v[c - 1]
        accs.append(jnp.sum(acc.reshape(16, 8, 128), axis=0))
    start_sum(1, load_row(accs))

    yd[...] = exact_dot(mats_v[2], state1)
    derived = exact_dot(mats_v[3], state1)
    for t in range(3):
        ds_[:, t] = derived[:, t * 128 : (t + 1) * 128].reshape(PEERS, 16, 128)
    peers(lambda p: deriv_out(p).start())
    dr[:, pl.ds(me, 1)] = ds_[pl.ds(me, 1)].reshape(3, 1, 16, 128)

    peers(lambda p: arrived(n1.at[pl.ds(1, 3), p], n_recv.at[p]))

    @pl.when(has_high)
    def _():
        pl.loop(0, 2)(lambda p: arrived(n1.at[4, p], h1_recv.at[p]))

    @pl.when(has_low)
    def _():
        pl.loop(PEERS - 2, PEERS)(lambda p: arrived(n1.at[0, p], h1_recv.at[p]))

    for column in range(NB + 2):
        slot = 2 * column + 6
        left, right = n1[slot // 8, slot % 8], n1[slot // 8, slot % 8 + 1]
        nf[column] = jnp.concatenate([left, right], axis=1)

    sweep_products(1, nf, base2, lambda: None)

    wait_base(1)
    spectrum = exact_dot(mats_v[0], wide(xb2)) + yd[...]
    final = wide(xs) + exact_dot(mats_v[1], spectrum * scal[...])
    for t in range(3):
        as_[:, t] = final[:, t * 128 : (t + 1) * 128].reshape(PEERS, 16, 128)
    peers(lambda p: adj_out(p).start())
    ar[:, pl.ds(me, 1)] = as_[pl.ds(me, 1)].reshape(3, 1, 16, 128)

    def put(out, fn):
        for q in range(24):
            value = fn(q // 8, q % 8)
            for i in range(OWN):
                out[i, :, q * 128 : (q + 1) * 128] = value[i * NOBJ : (i + 1) * NOBJ, :]

    peers(lambda p: arrived(dr.at[:, p], d_recv.at[p]))
    put(out_r, lambda t, p: base2[t, p] + dr[t, p])
    write_r = pltpu.make_async_copy(out_r, res_hbm, l_sem.at[0])
    write_r.start()
    peers(lambda p: arrived(ar.at[:, p], a_recv.at[p]))
    put(out_a, lambda t, p: ar[t, p])
    write_a = pltpu.make_async_copy(out_a, adj_hbm, l_sem.at[1])
    write_a.start()

    @pl.when(has_low)
    def _():
        halo0_low().wait_send()

    @pl.when(has_high)
    def _():
        halo0_high().wait_send()

    at_low(lambda p: halo1_low(p).wait_send())
    at_high(lambda p: halo1_high(p).wait_send())

    def drain(p):
        state_out(p).wait_send()
        narrow_out(p).wait_send()
        deriv_out(p).wait_send()
        adj_out(p).wait_send()
        for k in range(2):
            sum2_out(k, p).wait_send()
            for t in range(3):
                base_out(k, t, p).wait_send()

    peers(drain)

    def drain_span(q):
        for k in range(2):
            sum1_out(k, q).wait_send()

    spans(drain_span)
    write_r.wait()
    write_a.wait()


def solution(mesh):
    n_span = mesh.shape["span"]
    mats, harm = constants()

    def local(
        adjoint_start,
        source,
        jacobian_tiles,
        tile_columns,
        pseudo_time,
        control_terms,
        surface_rows,
        surface_weight,
        trim_inverse,
    ):
        any_spec = pl.BlockSpec(memory_space=pl.ANY)
        smem = pl.BlockSpec(memory_space=pltpu.SMEM)
        dma = pltpu.SemaphoreType.DMA
        vm = pltpu.VMEM
        out = jax.ShapeDtypeStruct((OWN, NOBJ, ROWS), F32)
        return pl.pallas_call(
            lambda *refs: kernel(n_span, *refs),
            out_shape=(out, out),
            in_specs=[smem, smem] + [any_spec] * 9,
            out_specs=(any_spec, any_spec),
            scratch_shapes=[
                vm((NB, OWN, K, TILE, TILE), BF16),
                vm((OWN, NOBJ, ROWS), F32),
                vm((OWN, NOBJ, ROWS), F32),
                vm((3, OWN, ROWS), F32),
                vm((3, 8, 128), F32),
                vm((6, 128), jnp.int32),
                vm((3, S_DEV), F32),
                vm((4, 128, 384), BF16),
                vm((2, 128, 128), F32),
                vm((OWN, NOBJ, ROWS), F32),
                vm((OWN, NOBJ, ROWS), F32),
                vm((3, 8, 16, 128), F32),
                vm((NB + 2, 16, TILE), BF16),
                vm((5, 8, 16, 128), BF16),
                vm((NB + 2, 16, TILE), BF16),
                vm((72, 128), F32),
                vm((3, 8, 16, 128), F32),
                vm((3, 8, 16, 128), F32),
                vm((8, 3, 16, 128), F32),
                vm((8, 3, 16, 128), F32),
                vm((8, 3, 16, 128), F32),
                vm((128, 384), F32),
                vm((128, 384), F32),
                vm((8, 3, 16, 128), BF16),
                vm((8, 3, 16, 128), F32),
                vm((3, 8, 16, 128), F32),
                vm((8, 3, 16, 128), F32),
                vm((3, 8, 16, 128), F32),
                vm((2, 1, 128), F32),
                vm((2, n_span, 1, 128), F32),
                vm((2, 1, 128), F32),
                vm((2, PEERS, 1, 128), F32),
                dma((NB,)),
                dma((8,)),
                dma((8,)),
                dma((8,)),
                dma((2,)),
                dma((2,)),
                dma((2, 3, 8)),
                dma((2, 3, 8)),
                dma((8,)),
                dma((8,)),
                dma((2, 8)),
                dma((8,)),
                dma((8,)),
                dma((8,)),
                dma((8,)),
                dma((8,)),
                dma((2, n_span)),
                dma((2, n_span)),
                dma((2, 8)),
                dma((2, 8)),
            ],
            compiler_params=pltpu.CompilerParams(
                collective_id=0, has_side_effects=True, vmem_limit_bytes=40 * 1024 * 1024
            ),
        )(
            tile_columns,
            trim_inverse,
            adjoint_start,
            source,
            jacobian_tiles,
            pseudo_time.reshape(3, 8, 128),
            control_terms,
            surface_rows.reshape(6, 128),
            surface_weight,
            jnp.asarray(mats),
            jnp.asarray(harm),
        )

    return jax.shard_map(
        local,
        mesh=mesh,
        in_specs=(
            P("inst", None, "span"),
            P("inst", None, "span"),
            P("inst", "span", None, None, None),
            P("span", None),
            P("span"),
            P(None, "inst", "span"),
            P("span"),
            P(),
            P(),
        ),
        out_specs=(P("inst", None, "span"), P("inst", None, "span")),
        check_vma=False,
    )
```

```python
import math

import jax
import jax.numpy as jnp
import ml_dtypes
import numpy as np
from jax import lax
from jax.experimental import pallas as pl
from jax.experimental.pallas import tpu as pltpu
from jax.sharding import PartitionSpec as P

MESH = pl.DeviceIdType.MESH
F32 = jnp.float32
BF16 = jnp.bfloat16

INST = 32
PEERS = 8
OWN = 4
NOBJ = 4
ROWS = 3072
NB = 12
K = 3
TILE = 256
S_DEV = 768
RATE = 0.25
RELAX = 0.8


def split_const(a):
    hi = a.astype(ml_dtypes.bfloat16)
    lo = (a - hi.astype(np.float64)).astype(ml_dtypes.bfloat16)
    return np.concatenate([hi, hi, lo], axis=-1)


def constants():
    theta = 2.0 * math.pi * np.arange(INST) / INST
    half = INST // 2
    trans = np.concatenate(
        [
            np.cos(np.arange(half + 1)[:, None] * theta[None, :]),
            np.sin(np.arange(1, half)[:, None] * theta[None, :]),
        ]
    )
    spread = theta[:, None] - theta[None, :]
    orders = np.arange(1, half)[:, None, None]
    deriv = -(2.0 / INST) * np.sum(orders * np.sin(orders * spread[None]), axis=0)
    eye = np.eye(NOBJ)
    forward = np.kron(trans, eye)
    back = np.kron(trans.T, eye)
    forward_deriv = RATE * np.kron(trans @ deriv, eye)
    own_deriv = RATE * np.kron(deriv, eye)
    mats = [forward, back, forward_deriv, own_deriv]
    for c in range(3):
        spread_c = np.zeros((128, PEERS, 4, OWN))
        spread_c[:, :, c, :] = np.repeat(trans, NOBJ, axis=0).reshape(128, PEERS, OWN)
        mats.append(spread_c.reshape(128, 128))
    mats = np.stack([split_const(m) for m in mats])
    angle = np.repeat(theta, NOBJ)
    harm = np.stack([np.cos(angle), np.sin(angle)]).astype(np.float32)
    harm = np.ascontiguousarray(np.broadcast_to(harm[:, :, None], (2, 128, 128)))
    return mats, harm


def exact_dot(mat, x):
    hi = x.astype(BF16)
    lo = (x - hi.astype(F32)).astype(BF16)
    return jnp.dot(mat, jnp.concatenate([hi, lo, hi], axis=0), preferred_element_type=F32)


def kernel(
    n_span,
    cols_ref,
    tinv_ref,
    state_hbm,
    source_hbm,
    jac_hbm,
    pt_hbm,
    ct_hbm,
    rows_hbm,
    sw_hbm,
    mats_hbm,
    harm_hbm,
    adj_hbm,
    res_hbm,
    jbuf,
    st_v,
    src_v,
    ct_v,
    pt_v,
    rows_v,
    sw_v,
    mats_v,
    harm_v,
    out_a,
    out_r,
    s0,
    n0,
    n1,
    nf,
    w_v,
    base1,
    base2,
    xs,
    xb1,
    xb2,
    scal,
    yd,
    ctf,
    st1,
    ns,
    ds_,
    dr,
    as_,
    ar,
    r1s,
    r1r,
    r2s,
    r2r,
    j_sem,
    l_sem,
    st_send,
    st_recv,
    h0_send,
    h0_recv,
    b_send,
    b_recv,
    n_send,
    n_recv,
    h1_send,
    h1_recv,
    d_send,
    d_recv,
    a_send,
    a_recv,
    r1_send,
    r1_recv,
    r2_send,
    r2_recv,
):
    me = lax.axis_index("inst")
    sp = lax.axis_index("span")
    last = n_span - 1

    zero2 = jnp.zeros((2, 16, 128), BF16)
    n1[0, 6:8] = zero2
    n1[4, 0:2] = zero2
    for column in (0, NB + 1):
        n0[column] = jnp.zeros((16, TILE), BF16)

    barrier = pltpu.get_barrier_semaphore()

    def signal(i, s):
        pl.semaphore_signal(barrier, inc=1, device_id=(i, s), device_id_type=MESH)

    def peers(fn):
        @pl.loop(1, PEERS)
        def _(d):
            fn(jnp.bitwise_xor(me, d))

    def far_first(fn):
        for d in (5, 4, 7, 6, 3, 2, 1):
            fn(jnp.bitwise_xor(me, d))

    def spans(fn):
        @pl.loop(1, n_span)
        def _(d):
            fn(lax.rem(sp + d, n_span))

    peers(lambda p: signal(p, sp))
    spans(lambda q: signal(me, q))

    has_low = sp > 0
    has_high = sp < last
    def at_low(fn):
        @pl.when(has_low)
        def _():
            @pl.when(me < 2)
            def _():
                pl.loop(0, PEERS)(fn)

    def at_high(fn):
        @pl.when(has_high)
        def _():
            @pl.when(me >= PEERS - 2)
            def _():
                pl.loop(0, PEERS)(fn)

    def around(p):
        signal(p, lax.rem(sp + 1, n_span))
        signal(p, lax.rem(sp + n_span - 1, n_span))

    peers(around)

    local_in = [
        (state_hbm, st_v),
        (rows_hbm, rows_v),
        (sw_hbm.at[:, pl.ds(pl.multiple_of(sp * S_DEV, S_DEV), S_DEV)], sw_v),
        (harm_hbm, harm_v),
        (ct_hbm, ct_v),
        (source_hbm, src_v),
        (pt_hbm, pt_v),
        (mats_hbm, mats_v),
    ]
    loads = [pltpu.make_async_copy(a, b, l_sem.at[n]) for n, (a, b) in enumerate(local_in)]
    for c in loads:
        c.start()

    def jac_copy(b):
        return pltpu.make_async_copy(jac_hbm.at[:, b], jbuf.at[b], j_sem.at[b])

    @pl.loop(0, NB)
    def _(b):
        jac_copy(b).start()

    loads[0].wait()
    flat = jnp.concatenate([st_v[i] for i in range(OWN)], axis=0)
    for q in range(24):
        piece = flat[:, q * 128 : (q + 1) * 128]
        s0[q // 8, q % 8, 0:16] = piece
    loads[4].wait()
    flat_c = jnp.concatenate([ct_v[c] for c in range(3)] + [jnp.zeros((OWN, ROWS), F32)], axis=0)
    for q in range(24):
        s0[q // 8, q % 8, 16:32] = flat_c[:, q * 128 : (q + 1) * 128]
    for b in range(NB):
        n0[b + 1] = flat[:, b * TILE : (b + 1) * TILE].astype(BF16)

    def to(src, dst, send, recv, i, s):
        return pltpu.make_async_remote_copy(
            src_ref=src, dst_ref=dst, send_sem=send, recv_sem=recv, device_id=(i, s), device_id_type=MESH
        )

    def halo0_low():
        return to(n0.at[1], n0.at[NB + 1], h0_send.at[0], h0_recv.at[0], me, sp - 1)

    def halo0_high():
        return to(n0.at[NB], n0.at[0], h0_send.at[1], h0_recv.at[1], me, sp + 1)

    def state_out(p):
        return to(s0.at[:, p], xs.at[me], st_send.at[0], st_recv.at[0], p, sp)

    def base_out(k, t, p):
        src, dst = (base1, xb1) if k == 0 else (base2, xb2)
        return to(src.at[t, p], dst.at[me, t], b_send.at[k], b_recv.at[k], p, sp)

    def narrow_out(p):
        return to(ns.at[p], n1.at[pl.ds(1, 3), me], n_send.at[0], n_recv.at[0], p, sp)

    def halo1_low(p):
        return to(ns.at[p, 0], n1.at[4, me], h1_send.at[0], h1_recv.at[0], p, sp - 1)

    def halo1_high(p):
        return to(ns.at[p, 2], n1.at[0, me], h1_send.at[1], h1_recv.at[1], p, sp + 1)

    def deriv_out(p):
        return to(ds_.at[p], dr.at[:, me], d_send.at[0], d_recv.at[0], p, sp)

    def adj_out(p):
        return to(as_.at[p], ar.at[:, me], a_send.at[0], a_recv.at[0], p, sp)

    def sum1_out(k, q):
        return to(r1s.at[k], r1r.at[k, sp], r1_send.at[k], r1_recv.at[k], me, q)

    def sum2_out(k, p):
        return to(r2s.at[k], r2r.at[k, me], r2_send.at[k], r2_recv.at[k], p, sp)

    def arrived(dst, sem):
        pltpu.make_async_copy(dst, dst, sem).wait()

    loads[1].wait()
    loads[2].wait()
    rows = jnp.concatenate([rows_v[q : q + 1, :] for q in range(6)], axis=1)
    high, low = lax.div(rows, 128), lax.rem(rows, 128)
    tiles24 = lax.broadcasted_iota(jnp.int32, (24, S_DEV), 0)
    hit = jnp.broadcast_to(high, (24, S_DEV)) == tiles24
    spread = jnp.concatenate(
        [jnp.where(hit, jnp.broadcast_to(sw_v[c : c + 1, :], (24, S_DEV)), 0.0) for c in range(3)], axis=0
    )
    spread_hi = spread.astype(BF16)
    spread_lo = (spread - spread_hi.astype(F32)).astype(BF16)
    lane_hit = jnp.broadcast_to(low, (128, S_DEV)) == lax.broadcasted_iota(jnp.int32, (128, S_DEV), 0)
    lane_hit = jnp.where(lane_hit, 1.0, 0.0).astype(BF16)
    nt = (((1,), (1,)), ((), ()))
    w_v[...] = lax.dot_general(spread_hi, lane_hit, nt, preferred_element_type=F32) + lax.dot_general(
        spread_lo, lane_hit, nt, preferred_element_type=F32
    )

    lane8 = lax.broadcasted_iota(jnp.int32, (8, 128), 1)
    row8 = lax.rem(lax.broadcasted_iota(jnp.int32, (8, 128), 0), NOBJ)

    def load_row(accs):
        total = jnp.zeros((8, 128), F32)
        for c in range(3):
            col = jnp.sum(accs[c], axis=1, keepdims=True)
            total = total + jnp.where(lane8 == c * NOBJ + row8, jnp.broadcast_to(col, (8, 128)), 0.0)
        return jnp.sum(total, axis=0, keepdims=True)

    loads[3].wait()
    accs = []
    for c in range(3):
        acc = jnp.zeros((16, 128), F32)
        for q in range(24):
            acc = acc + s0[q // 8, q % 8, 0:16] * jnp.broadcast_to(w_v[c * 24 + q : c * 24 + q + 1, :], (16, 128))
        if c > 0:
            acc = acc * harm_v[c - 1, pl.ds(pl.multiple_of(me * 16, 16), 16), :]
        accs.append(acc[0:8] + acc[8:16])

    first_row = load_row(accs)
    pl.semaphore_wait(barrier, 3 * (PEERS - 1) + n_span - 1)

    @pl.when(has_low)
    def _():
        halo0_low().start()

    @pl.when(has_high)
    def _():
        halo0_high().start()

    def start_sum(k, row):
        r1s[k] = row
        r1r[k, pl.ds(sp, 1)] = row.reshape(1, 1, 128)
        spans(lambda q: sum1_out(k, q).start())

    start_sum(0, first_row)
    far_first(lambda p: state_out(p).start())
    xs[pl.ds(me, 1)] = s0[:, pl.ds(me, 1)].reshape(1, 3, 32, 128)

    def middle_sum(k):
        arrived(r1r.at[k, pl.ds(0, n_span - 1)], r1_recv.at[k])
        row = jnp.sum(r1r[k], axis=0)
        r2s[k] = row
        r2r[k, pl.ds(me, 1)] = row.reshape(1, 1, 128)
        far_first(lambda p: sum2_out(k, p).start())

    def multiplier(k):
        arrived(r2r.at[k, pl.ds(0, PEERS - 1)], r2_recv.at[k])
        row = jnp.broadcast_to(jnp.sum(r2r[k], axis=0), (8, 128))
        out = []
        for c in range(3):
            mask = jnp.zeros((8, 128), F32)
            for d in range(3):
                mask = jnp.where(lane8 == d * NOBJ + row8, tinv_ref[c, d], mask)
            col = jnp.sum(row * mask, axis=1, keepdims=True)
            out.append(jnp.broadcast_to(col, (8, 128)))
        return out

    inst_row = lax.div(lax.broadcasted_iota(jnp.int32, (16, TILE), 0), NOBJ)
    masks = [jnp.where(inst_row == i, 1.0, 0.0).astype(BF16) for i in range(OWN)]

    def product(b, narrow, base):
        blocks = [narrow[cols_ref[k, b] + 1] for k in range(K)]
        left = jnp.concatenate([blocks[k] * masks[i] for i in range(OWN) for k in range(K)], axis=1)
        acc = jnp.dot(left, jbuf[b].reshape(OWN * K * TILE, TILE), preferred_element_type=F32)
        rows = jnp.concatenate([src_v[i, :, b * TILE : (b + 1) * TILE] for i in range(OWN)], axis=0)
        value = rows - acc
        for half in range(2):
            q = 2 * b + half
            base[q // 8, q % 8] = value[:, half * 128 : (half + 1) * 128]

    def sweep_products(k, narrow, base, landed):
        for t in range(3):
            for b in range(4 * t, 4 * t + 4):
                if k == 0:
                    jac_copy(b).wait()
                product(b, narrow, base)
            far_first(lambda p: base_out(k, t, p).start())
            landed[pl.ds(me, 1), t] = base[t, pl.ds(me, 1)]
            if t == k:
                middle_sum(k)

    def wide(ref):
        return jnp.concatenate([ref[:, t].reshape(128, 128) for t in range(3)], axis=1)

    def wide_part(ref, first):
        parts = [ref[:, t, first : first + 16].reshape(128, 128) for t in range(3)]
        return jnp.concatenate(parts, axis=1)

    def add_control(k):
        mult = multiplier(k)
        total = yd[...].reshape(16, 8, 384)
        for c in range(3):
            total = total - ctf[c].reshape(16, 8, 384) * jnp.concatenate([mult[c]] * 3, axis=1)[None]
        yd[...] = total.reshape(128, 384)
        return mult

    @pl.when(has_high)
    def _():
        arrived(n0.at[NB + 1], h0_recv.at[0])

    @pl.when(has_low)
    def _():
        arrived(n0.at[0], h0_recv.at[1])

    loads[5].wait()
    sweep_products(0, n0, base1, xb1)

    for c in loads[6:]:
        c.wait()
    order = lax.div(lax.broadcasted_iota(jnp.int32, (128, 128), 0), NOBJ)
    freq = jnp.where(order > INST // 2, order - INST // 2, order)
    ends = jnp.logical_or(freq == 0, freq == INST // 2)
    weight = jnp.where(ends, RELAX / INST, 2.0 * RELAX / INST)
    offset = RATE * freq.astype(F32)
    for t in range(3):
        pt = jnp.broadcast_to(pt_v[t, pl.ds(me, 1), :], (128, 128))
        scal[:, t * 128 : (t + 1) * 128] = weight / (pt + offset)
    arrived(xs.at[pl.ds(0, PEERS - 1)], st_recv.at[0])
    state0 = wide_part(xs, 0)
    yd[...] = exact_dot(mats_v[2], state0)
    control = wide_part(xs, 16)
    for c in range(3):
        ctf[c] = exact_dot(mats_v[4 + c], control)
    add_control(0)

    def wait_base(k):
        arrived((xb1 if k == 0 else xb2).at[pl.ds(0, PEERS - 1)], b_recv.at[k])

    wait_base(0)
    spectrum = exact_dot(mats_v[0], wide(xb1)) + yd[...]
    state1 = wide_part(xs, 0) + exact_dot(mats_v[1], spectrum * scal[...])
    st1[...] = state1
    for t in range(3):
        piece = state1[:, t * 128 : (t + 1) * 128]
        ns[:, t] = piece.astype(BF16).reshape(PEERS, 16, 128)
    far_first(lambda p: narrow_out(p).start())

    at_low(lambda p: halo1_low(p).start())
    at_high(lambda p: halo1_high(p).start())

    n1[pl.ds(1, 3), pl.ds(me, 1)] = ns[pl.ds(me, 1)].reshape(3, 1, 16, 128)

    accs = []
    for c in range(3):
        acc = jnp.zeros((128, 128), F32)
        for t in range(3):
            weight = w_v[pl.ds(c * 24 + t * 8 + me, 1), :]
            acc = acc + state1[:, t * 128 : (t + 1) * 128] * jnp.broadcast_to(weight, (128, 128))
        if c > 0:
            acc = acc * harm_v[c - 1]
        accs.append(jnp.sum(acc.reshape(16, 8, 128), axis=0))
    start_sum(1, load_row(accs))

    yd[...] = exact_dot(mats_v[2], state1)
    derived = exact_dot(mats_v[3], state1)
    for t in range(3):
        ds_[:, t] = derived[:, t * 128 : (t + 1) * 128].reshape(PEERS, 16, 128)
    far_first(lambda p: deriv_out(p).start())
    dr[:, pl.ds(me, 1)] = ds_[pl.ds(me, 1)].reshape(3, 1, 16, 128)

    arrived(n1.at[pl.ds(1, 3), pl.ds(0, PEERS - 1)], n_recv.at[0])

    @pl.when(has_high)
    def _():
        arrived(n1.at[4, pl.ds(0, 2)], h1_recv.at[0])

    @pl.when(has_low)
    def _():
        arrived(n1.at[0, pl.ds(PEERS - 2, 2)], h1_recv.at[1])

    for column in range(NB + 2):
        slot = 2 * column + 6
        left, right = n1[slot // 8, slot % 8], n1[slot // 8, slot % 8 + 1]
        nf[column] = jnp.concatenate([left, right], axis=1)

    sweep_products(1, nf, base2, xb2)
    mult = add_control(1)

    wait_base(1)
    spectrum = exact_dot(mats_v[0], wide(xb2)) + yd[...]
    final = st1[...] + exact_dot(mats_v[1], spectrum * scal[...])
    for t in range(3):
        as_[:, t] = final[:, t * 128 : (t + 1) * 128].reshape(PEERS, 16, 128)
    far_first(lambda p: adj_out(p).start())
    ar[:, pl.ds(me, 1)] = as_[pl.ds(me, 1)].reshape(3, 1, 16, 128)

    def drain():
        @pl.when(has_low)
        def _():
            halo0_low().wait_send()

        @pl.when(has_high)
        def _():
            halo0_high().wait_send()

        @pl.when(has_low)
        def _():
            @pl.when(me < 2)
            def _():
                arrived(ns.at[:, 0], h1_send.at[0])

        @pl.when(has_high)
        def _():
            @pl.when(me >= PEERS - 2)
            def _():
                arrived(ns.at[:, 2], h1_send.at[1])

        arrived(s0.at[:, pl.ds(0, PEERS - 1)], st_send.at[0])
        arrived(ns.at[pl.ds(0, PEERS - 1)], n_send.at[0])
        arrived(ds_.at[pl.ds(0, PEERS - 1)], d_send.at[0])
        for k, base in ((0, base1), (1, base2)):
            arrived(base.at[:, pl.ds(0, PEERS - 1)], b_send.at[k])
            arrived(r1r.at[k, pl.ds(0, n_span - 1)], r1_send.at[k])
            arrived(r2r.at[k, pl.ds(0, PEERS - 1)], r2_send.at[k])

    def put(out, fn):
        for q in range(24):
            value = fn(q // 8, q % 8)
            for i in range(OWN):
                out[i, :, q * 128 : (q + 1) * 128] = value[i * NOBJ : (i + 1) * NOBJ, :]

    mult16 = [jnp.concatenate([m, m], axis=0) for m in mult]
    first_half = lax.div(lax.broadcasted_iota(jnp.int32, (8, 128), 0), NOBJ) == 0

    def residual_tile(t, p):
        q = t * 8 + p
        lanes = slice(q * 128, (q + 1) * 128)
        value = base2[t, p] + dr[t, p]
        for c in range(3):
            parts = []
            for h in range(2):
                first = jnp.broadcast_to(ct_v[c, 2 * h : 2 * h + 1, lanes], (8, 128))
                second = jnp.broadcast_to(ct_v[c, 2 * h + 1 : 2 * h + 2, lanes], (8, 128))
                parts.append(jnp.where(first_half, first, second))
            value = value - jnp.concatenate(parts, axis=0) * mult16[c]
        return value

    arrived(dr.at[:, pl.ds(0, PEERS - 1)], d_recv.at[0])
    put(out_r, residual_tile)
    write_r = pltpu.make_async_copy(out_r, res_hbm, l_sem.at[0])
    write_r.start()
    drain()
    arrived(ar.at[:, pl.ds(0, PEERS - 1)], a_recv.at[0])
    put(out_a, lambda t, p: ar[t, p])
    write_a = pltpu.make_async_copy(out_a, adj_hbm, l_sem.at[1])
    write_a.start()

    arrived(as_.at[pl.ds(0, PEERS - 1)], a_send.at[0])
    write_r.wait()
    write_a.wait()


def solution(mesh):
    n_span = mesh.shape["span"]
    mats, harm = constants()

    def local(
        adjoint_start,
        source,
        jacobian_tiles,
        tile_columns,
        pseudo_time,
        control_terms,
        surface_rows,
        surface_weight,
        trim_inverse,
    ):
        any_spec = pl.BlockSpec(memory_space=pl.ANY)
        smem = pl.BlockSpec(memory_space=pltpu.SMEM)
        dma = pltpu.SemaphoreType.DMA
        vm = pltpu.VMEM
        out = jax.ShapeDtypeStruct((OWN, NOBJ, ROWS), F32)
        return pl.pallas_call(
            lambda *refs: kernel(n_span, *refs),
            out_shape=(out, out),
            in_specs=[smem, smem] + [any_spec] * 9,
            out_specs=(any_spec, any_spec),
            scratch_shapes=[
                vm((NB, OWN, K, TILE, TILE), BF16),
                vm((OWN, NOBJ, ROWS), F32),
                vm((OWN, NOBJ, ROWS), F32),
                vm((3, OWN, ROWS), F32),
                vm((3, 8, 128), F32),
                vm((6, 128), jnp.int32),
                vm((3, S_DEV), F32),
                vm((7, 128, 384), BF16),
                vm((2, 128, 128), F32),
                vm((OWN, NOBJ, ROWS), F32),
                vm((OWN, NOBJ, ROWS), F32),
                vm((3, 8, 32, 128), F32),
                vm((NB + 2, 16, TILE), BF16),
                vm((5, 8, 16, 128), BF16),
                vm((NB + 2, 16, TILE), BF16),
                vm((72, 128), F32),
                vm((3, 8, 16, 128), F32),
                vm((3, 8, 16, 128), F32),
                vm((8, 3, 32, 128), F32),
                vm((8, 3, 16, 128), F32),
                vm((8, 3, 16, 128), F32),
                vm((128, 384), F32),
                vm((128, 384), F32),
                vm((3, 128, 384), F32),
                vm((128, 384), F32),
                vm((8, 3, 16, 128), BF16),
                vm((8, 3, 16, 128), F32),
                vm((3, 8, 16, 128), F32),
                vm((8, 3, 16, 128), F32),
                vm((3, 8, 16, 128), F32),
                vm((2, 1, 128), F32),
                vm((2, n_span, 1, 128), F32),
                vm((2, 1, 128), F32),
                vm((2, PEERS, 1, 128), F32),
                dma((NB,)),
                dma((8,)),
                dma((1,)),
                dma((1,)),
                dma((2,)),
                dma((2,)),
                dma((2,)),
                dma((2,)),
                dma((1,)),
                dma((1,)),
                dma((2,)),
                dma((2,)),
                dma((1,)),
                dma((1,)),
                dma((1,)),
                dma((1,)),
                dma((2,)),
                dma((2,)),
                dma((2,)),
                dma((2,)),
            ],
            compiler_params=pltpu.CompilerParams(
                collective_id=0, has_side_effects=True, vmem_limit_bytes=62 * 1024 * 1024
            ),
        )(
            tile_columns.T,
            trim_inverse,
            adjoint_start,
            source,
            jacobian_tiles,
            pseudo_time.reshape(3, 8, 128),
            control_terms,
            surface_rows.reshape(6, 128),
            surface_weight,
            jnp.asarray(mats),
            jnp.asarray(harm),
        )

    return jax.shard_map(
        local,
        mesh=mesh,
        in_specs=(
            P("inst", None, "span"),
            P("inst", None, "span"),
            P("inst", "span", None, None, None),
            P("span", None),
            P("span"),
            P(None, "inst", "span"),
            P("span"),
            P(),
            P(),
        ),
        out_specs=(P("inst", None, "span"), P("inst", None, "span")),
        check_vma=False,
    )
```

```python
import math

import jax
import jax.numpy as jnp
import ml_dtypes
import numpy as np
from jax import lax
from jax.experimental import pallas as pl
from jax.experimental.pallas import tpu as pltpu
from jax.sharding import PartitionSpec as P

MESH = pl.DeviceIdType.MESH
F32 = jnp.float32
BF16 = jnp.bfloat16

INST = 32
PEERS = 8
OWN = 4
NOBJ = 4
ROWS = 3072
NB = 12
K = 3
TILE = 256
S_DEV = 768
RATE = 0.25
RELAX = 0.8


def split_const(a):
    hi = a.astype(ml_dtypes.bfloat16)
    lo = (a - hi.astype(np.float64)).astype(ml_dtypes.bfloat16)
    return np.concatenate([hi, hi, lo], axis=-1)


def constants():
    theta = 2.0 * math.pi * np.arange(INST) / INST
    half = INST // 2
    trans = np.concatenate(
        [
            np.cos(np.arange(half + 1)[:, None] * theta[None, :]),
            np.sin(np.arange(1, half)[:, None] * theta[None, :]),
        ]
    )
    spread = theta[:, None] - theta[None, :]
    orders = np.arange(1, half)[:, None, None]
    deriv = -(2.0 / INST) * np.sum(orders * np.sin(orders * spread[None]), axis=0)
    eye = np.eye(NOBJ)
    forward = np.kron(trans, eye)
    back = np.kron(trans.T, eye)
    forward_deriv = RATE * np.kron(trans @ deriv, eye)
    own_deriv = RATE * np.kron(deriv, eye)
    mats = [forward, back, forward_deriv, own_deriv]
    for c in range(3):
        spread_c = np.zeros((128, PEERS, 4, OWN))
        spread_c[:, :, c, :] = np.repeat(trans, NOBJ, axis=0).reshape(128, PEERS, OWN)
        mats.append(spread_c.reshape(128, 128))
    mats = np.stack([split_const(m) for m in mats])
    angle = np.repeat(theta, NOBJ)
    harm = np.stack([np.cos(angle), np.sin(angle)]).astype(np.float32)
    harm = np.ascontiguousarray(np.broadcast_to(harm[:, :, None], (2, 128, 128)))
    return mats, harm


def exact_dot(mat, x):
    hi = x.astype(BF16)
    lo = (x - hi.astype(F32)).astype(BF16)
    return jnp.dot(mat, jnp.concatenate([hi, lo, hi], axis=0), preferred_element_type=F32)


def kernel(
    n_span,
    cols_ref,
    tinv_ref,
    state_hbm,
    source_hbm,
    jac_hbm,
    pt_hbm,
    ct_hbm,
    rows_hbm,
    sw_hbm,
    mats_hbm,
    harm_hbm,
    adj_hbm,
    res_hbm,
    jbuf,
    st_v,
    src_v,
    ct_v,
    pt_v,
    rows_v,
    sw_v,
    mats_v,
    harm_v,
    out_a,
    out_r,
    s0,
    n0,
    n1,
    nf,
    w_v,
    base1,
    base2,
    xs,
    xb1,
    xb2,
    scal,
    yd,
    ctf,
    st1,
    ns,
    ds_,
    dr,
    as_,
    ar,
    r1s,
    r1r,
    r2s,
    r2r,
    j_sem,
    l_sem,
    st_send,
    st_recv,
    h0_send,
    h0_recv,
    b_send,
    b_recv,
    n_send,
    n_recv,
    h1_send,
    h1_recv,
    d_send,
    d_recv,
    a_send,
    a_recv,
    r1_send,
    r1_recv,
    r2_send,
    r2_recv,
):
    me = lax.axis_index("inst")
    sp = lax.axis_index("span")
    last = n_span - 1

    local_in = [
        (state_hbm, st_v),
        (rows_hbm, rows_v),
        (sw_hbm.at[:, pl.ds(pl.multiple_of(sp * S_DEV, S_DEV), S_DEV)], sw_v),
        (harm_hbm, harm_v),
        (ct_hbm, ct_v),
        (source_hbm, src_v),
        (pt_hbm, pt_v),
        (mats_hbm, mats_v),
    ]
    loads = [pltpu.make_async_copy(a, b, l_sem.at[n]) for n, (a, b) in enumerate(local_in)]
    for c in loads:
        c.start()

    def jac_copy(b):
        return pltpu.make_async_copy(jac_hbm.at[:, b], jbuf.at[b], j_sem.at[b])

    @pl.loop(0, NB)
    def _(b):
        jac_copy(b).start()

    zero2 = jnp.zeros((2, 16, 128), BF16)
    n1[0, 6:8] = zero2
    n1[4, 0:2] = zero2
    for column in (0, NB + 1):
        n0[column] = jnp.zeros((16, TILE), BF16)

    barrier = pltpu.get_barrier_semaphore()

    def signal(i, s):
        pl.semaphore_signal(barrier, inc=1, device_id=(i, s), device_id_type=MESH)

    def peers(fn):
        @pl.loop(1, PEERS)
        def _(d):
            fn(jnp.bitwise_xor(me, d))

    def far_first(fn):
        for d in (5, 4, 7, 6, 3, 2, 1):
            fn(jnp.bitwise_xor(me, d))

    def spans(fn):
        @pl.loop(1, n_span)
        def _(d):
            fn(lax.rem(sp + d, n_span))

    peers(lambda p: signal(p, sp))
    spans(lambda q: signal(me, q))

    has_low = sp > 0
    has_high = sp < last
    def at_low(fn):
        @pl.when(has_low)
        def _():
            @pl.when(me < 2)
            def _():
                pl.loop(0, PEERS)(fn)

    def at_high(fn):
        @pl.when(has_high)
        def _():
            @pl.when(me >= PEERS - 2)
            def _():
                pl.loop(0, PEERS)(fn)

    def around(p):
        signal(p, lax.rem(sp + 1, n_span))
        signal(p, lax.rem(sp + n_span - 1, n_span))

    peers(around)

    loads[0].wait()
    flat = jnp.concatenate([st_v[i] for i in range(OWN)], axis=0)
    for q in range(24):
        piece = flat[:, q * 128 : (q + 1) * 128]
        s0[q // 8, q % 8, 0:16] = piece
    loads[4].wait()
    flat_c = jnp.concatenate([ct_v[c] for c in range(3)] + [jnp.zeros((OWN, ROWS), F32)], axis=0)
    for q in range(24):
        s0[q // 8, q % 8, 16:32] = flat_c[:, q * 128 : (q + 1) * 128]
    for b in range(NB):
        n0[b + 1] = flat[:, b * TILE : (b + 1) * TILE].astype(BF16)

    pl.semaphore_wait(barrier, 3 * (PEERS - 1) + n_span - 1)

    def to(src, dst, send, recv, i, s):
        return pltpu.make_async_remote_copy(
            src_ref=src, dst_ref=dst, send_sem=send, recv_sem=recv, device_id=(i, s), device_id_type=MESH
        )

    def halo0_low():
        return to(n0.at[1], n0.at[NB + 1], h0_send.at[0], h0_recv.at[0], me, sp - 1)

    def halo0_high():
        return to(n0.at[NB], n0.at[0], h0_send.at[1], h0_recv.at[1], me, sp + 1)

    def state_out(p):
        return to(s0.at[:, p], xs.at[me], st_send.at[0], st_recv.at[0], p, sp)

    def base_out(k, t, p):
        src, dst = (base1, xb1) if k == 0 else (base2, xb2)
        return to(src.at[t, p], dst.at[me, t], b_send.at[k], b_recv.at[k], p, sp)

    def narrow_out(p):
        return to(ns.at[p], n1.at[pl.ds(1, 3), me], n_send.at[0], n_recv.at[0], p, sp)

    def halo1_low(p):
        return to(ns.at[p, 0], n1.at[4, me], h1_send.at[0], h1_recv.at[0], p, sp - 1)

    def halo1_high(p):
        return to(ns.at[p, 2], n1.at[0, me], h1_send.at[1], h1_recv.at[1], p, sp + 1)

    def deriv_out(p):
        return to(ds_.at[p], dr.at[:, me], d_send.at[0], d_recv.at[0], p, sp)

    def adj_out(p):
        return to(as_.at[p], ar.at[:, me], a_send.at[0], a_recv.at[0], p, sp)

    def sum1_out(k, q):
        return to(r1s.at[k], r1r.at[k, sp], r1_send.at[k], r1_recv.at[k], me, q)

    def sum2_out(k, p):
        return to(r2s.at[k], r2r.at[k, me], r2_send.at[k], r2_recv.at[k], p, sp)

    def arrived(dst, sem):
        pltpu.make_async_copy(dst, dst, sem).wait()

    @pl.when(has_low)
    def _():
        halo0_low().start()

    @pl.when(has_high)
    def _():
        halo0_high().start()

    loads[1].wait()
    loads[2].wait()
    rows = jnp.concatenate([rows_v[q : q + 1, :] for q in range(6)], axis=1)
    high, low = lax.div(rows, 128), lax.rem(rows, 128)
    tiles24 = lax.broadcasted_iota(jnp.int32, (24, S_DEV), 0)
    hit = jnp.broadcast_to(high, (24, S_DEV)) == tiles24
    spread = jnp.concatenate(
        [jnp.where(hit, jnp.broadcast_to(sw_v[c : c + 1, :], (24, S_DEV)), 0.0) for c in range(3)], axis=0
    )
    spread_hi = spread.astype(BF16)
    spread_lo = (spread - spread_hi.astype(F32)).astype(BF16)
    lane_hit = jnp.broadcast_to(low, (128, S_DEV)) == lax.broadcasted_iota(jnp.int32, (128, S_DEV), 0)
    lane_hit = jnp.where(lane_hit, 1.0, 0.0).astype(BF16)
    nt = (((1,), (1,)), ((), ()))
    w_v[...] = lax.dot_general(spread_hi, lane_hit, nt, preferred_element_type=F32) + lax.dot_general(
        spread_lo, lane_hit, nt, preferred_element_type=F32
    )

    lane8 = lax.broadcasted_iota(jnp.int32, (8, 128), 1)
    row8 = lax.rem(lax.broadcasted_iota(jnp.int32, (8, 128), 0), NOBJ)

    def load_row(accs):
        total = jnp.zeros((8, 128), F32)
        for c in range(3):
            col = jnp.sum(accs[c], axis=1, keepdims=True)
            total = total + jnp.where(lane8 == c * NOBJ + row8, jnp.broadcast_to(col, (8, 128)), 0.0)
        return jnp.sum(total, axis=0, keepdims=True)

    loads[3].wait()
    accs = []
    for c in range(3):
        acc = jnp.zeros((16, 128), F32)
        for q in range(24):
            acc = acc + s0[q // 8, q % 8, 0:16] * jnp.broadcast_to(w_v[c * 24 + q : c * 24 + q + 1, :], (16, 128))
        if c > 0:
            acc = acc * harm_v[c - 1, pl.ds(pl.multiple_of(me * 16, 16), 16), :]
        accs.append(acc[0:8] + acc[8:16])

    def start_sum(k, row):
        r1s[k] = row
        r1r[k, pl.ds(sp, 1)] = row.reshape(1, 1, 128)
        spans(lambda q: sum1_out(k, q).start())

    start_sum(0, load_row(accs))
    far_first(lambda p: state_out(p).start())
    xs[pl.ds(me, 1)] = s0[:, pl.ds(me, 1)].reshape(1, 3, 32, 128)

    def middle_sum(k):
        arrived(r1r.at[k, pl.ds(0, n_span - 1)], r1_recv.at[k])
        row = jnp.sum(r1r[k], axis=0)
        r2s[k] = row
        r2r[k, pl.ds(me, 1)] = row.reshape(1, 1, 128)
        far_first(lambda p: sum2_out(k, p).start())

    def multiplier(k):
        arrived(r2r.at[k, pl.ds(0, PEERS - 1)], r2_recv.at[k])
        row = jnp.broadcast_to(jnp.sum(r2r[k], axis=0), (8, 128))
        out = []
        for c in range(3):
            mask = jnp.zeros((8, 128), F32)
            for d in range(3):
                mask = jnp.where(lane8 == d * NOBJ + row8, tinv_ref[c, d], mask)
            col = jnp.sum(row * mask, axis=1, keepdims=True)
            out.append(jnp.broadcast_to(col, (8, 128)))
        return out

    inst_row = lax.div(lax.broadcasted_iota(jnp.int32, (16, TILE), 0), NOBJ)
    masks = [jnp.where(inst_row == i, 1.0, 0.0).astype(BF16) for i in range(OWN)]

    def product(b, narrow, base):
        blocks = [narrow[cols_ref[k, b] + 1] for k in range(K)]
        left = jnp.concatenate([blocks[k] * masks[i] for i in range(OWN) for k in range(K)], axis=1)
        acc = jnp.dot(left, jbuf[b].reshape(OWN * K * TILE, TILE), preferred_element_type=F32)
        rows = jnp.concatenate([src_v[i, :, b * TILE : (b + 1) * TILE] for i in range(OWN)], axis=0)
        value = rows - acc
        for half in range(2):
            q = 2 * b + half
            base[q // 8, q % 8] = value[:, half * 128 : (half + 1) * 128]

    def sweep_products(k, narrow, base, landed):
        for t in range(3):
            for b in range(4 * t, 4 * t + 4):
                if k == 0:
                    jac_copy(b).wait()
                product(b, narrow, base)
            far_first(lambda p: base_out(k, t, p).start())
            landed[pl.ds(me, 1), t] = base[t, pl.ds(me, 1)]
            if t == 2 - k:
                middle_sum(k)

    def wide(ref):
        return jnp.concatenate([ref[:, t].reshape(128, 128) for t in range(3)], axis=1)

    def wide_part(ref, first):
        parts = [ref[:, t, first : first + 16].reshape(128, 128) for t in range(3)]
        return jnp.concatenate(parts, axis=1)

    def add_control(k):
        mult = multiplier(k)
        total = yd[...].reshape(16, 8, 384)
        for c in range(3):
            total = total - ctf[c].reshape(16, 8, 384) * jnp.concatenate([mult[c]] * 3, axis=1)[None]
        yd[...] = total.reshape(128, 384)
        return mult

    @pl.when(has_high)
    def _():
        arrived(n0.at[NB + 1], h0_recv.at[0])

    @pl.when(has_low)
    def _():
        arrived(n0.at[0], h0_recv.at[1])

    loads[5].wait()
    sweep_products(0, n0, base1, xb1)

    for c in loads[6:]:
        c.wait()
    order = lax.div(lax.broadcasted_iota(jnp.int32, (128, 128), 0), NOBJ)
    freq = jnp.where(order > INST // 2, order - INST // 2, order)
    ends = jnp.logical_or(freq == 0, freq == INST // 2)
    weight = jnp.where(ends, RELAX / INST, 2.0 * RELAX / INST)
    offset = RATE * freq.astype(F32)
    for t in range(3):
        pt = jnp.broadcast_to(pt_v[t, pl.ds(me, 1), :], (128, 128))
        scal[:, t * 128 : (t + 1) * 128] = weight / (pt + offset)
    arrived(xs.at[pl.ds(0, PEERS - 1)], st_recv.at[0])
    state0 = wide_part(xs, 0)
    yd[...] = exact_dot(mats_v[2], state0)
    control = wide_part(xs, 16)
    for c in range(3):
        ctf[c] = exact_dot(mats_v[4 + c], control)
    add_control(0)

    def wait_base(k):
        arrived((xb1 if k == 0 else xb2).at[pl.ds(0, PEERS - 1)], b_recv.at[k])

    wait_base(0)
    spectrum = exact_dot(mats_v[0], wide(xb1)) + yd[...]
    state1 = wide_part(xs, 0) + exact_dot(mats_v[1], spectrum * scal[...])
    st1[...] = state1
    for t in range(3):
        piece = state1[:, t * 128 : (t + 1) * 128]
        ns[:, t] = piece.astype(BF16).reshape(PEERS, 16, 128)
    far_first(lambda p: narrow_out(p).start())

    at_low(lambda p: halo1_low(p).start())
    at_high(lambda p: halo1_high(p).start())

    n1[pl.ds(1, 3), pl.ds(me, 1)] = ns[pl.ds(me, 1)].reshape(3, 1, 16, 128)

    accs = []
    for c in range(3):
        acc = jnp.zeros((128, 128), F32)
        for t in range(3):
            weight = w_v[pl.ds(c * 24 + t * 8 + me, 1), :]
            acc = acc + state1[:, t * 128 : (t + 1) * 128] * jnp.broadcast_to(weight, (128, 128))
        if c > 0:
            acc = acc * harm_v[c - 1]
        accs.append(jnp.sum(acc.reshape(16, 8, 128), axis=0))
    start_sum(1, load_row(accs))

    yd[...] = exact_dot(mats_v[2], state1)
    derived = exact_dot(mats_v[3], state1)
    for t in range(3):
        ds_[:, t] = derived[:, t * 128 : (t + 1) * 128].reshape(PEERS, 16, 128)
    far_first(lambda p: deriv_out(p).start())
    dr[:, pl.ds(me, 1)] = ds_[pl.ds(me, 1)].reshape(3, 1, 16, 128)

    arrived(n1.at[pl.ds(1, 3), pl.ds(0, PEERS - 1)], n_recv.at[0])

    @pl.when(has_high)
    def _():
        arrived(n1.at[4, pl.ds(0, 2)], h1_recv.at[0])

    @pl.when(has_low)
    def _():
        arrived(n1.at[0, pl.ds(PEERS - 2, 2)], h1_recv.at[1])

    for column in range(NB + 2):
        slot = 2 * column + 6
        left, right = n1[slot // 8, slot % 8], n1[slot // 8, slot % 8 + 1]
        nf[column] = jnp.concatenate([left, right], axis=1)

    sweep_products(1, nf, base2, xb2)
    mult = add_control(1)

    wait_base(1)
    spectrum = exact_dot(mats_v[0], wide(xb2)) + yd[...]
    final = st1[...] + exact_dot(mats_v[1], spectrum * scal[...])
    for t in range(3):
        as_[:, t] = final[:, t * 128 : (t + 1) * 128].reshape(PEERS, 16, 128)
    far_first(lambda p: adj_out(p).start())
    ar[:, pl.ds(me, 1)] = as_[pl.ds(me, 1)].reshape(3, 1, 16, 128)

    def drain():
        @pl.when(has_low)
        def _():
            halo0_low().wait_send()

        @pl.when(has_high)
        def _():
            halo0_high().wait_send()

        @pl.when(has_low)
        def _():
            @pl.when(me < 2)
            def _():
                arrived(ns.at[:, 0], h1_send.at[0])

        @pl.when(has_high)
        def _():
            @pl.when(me >= PEERS - 2)
            def _():
                arrived(ns.at[:, 2], h1_send.at[1])

        arrived(s0.at[:, pl.ds(0, PEERS - 1)], st_send.at[0])
        arrived(ns.at[pl.ds(0, PEERS - 1)], n_send.at[0])
        arrived(ds_.at[pl.ds(0, PEERS - 1)], d_send.at[0])
        for k, base in ((0, base1), (1, base2)):
            arrived(base.at[:, pl.ds(0, PEERS - 1)], b_send.at[k])
            arrived(r1r.at[k, pl.ds(0, n_span - 1)], r1_send.at[k])
            arrived(r2r.at[k, pl.ds(0, PEERS - 1)], r2_send.at[k])

    def put(out, fn):
        for q in range(24):
            value = fn(q // 8, q % 8)
            for i in range(OWN):
                out[i, :, q * 128 : (q + 1) * 128] = value[i * NOBJ : (i + 1) * NOBJ, :]

    mult16 = [jnp.concatenate([m, m], axis=0) for m in mult]
    first_half = lax.div(lax.broadcasted_iota(jnp.int32, (8, 128), 0), NOBJ) == 0

    def residual_tile(t, p):
        q = t * 8 + p
        lanes = slice(q * 128, (q + 1) * 128)
        value = base2[t, p] + dr[t, p]
        for c in range(3):
            parts = []
            for h in range(2):
                first = jnp.broadcast_to(ct_v[c, 2 * h : 2 * h + 1, lanes], (8, 128))
                second = jnp.broadcast_to(ct_v[c, 2 * h + 1 : 2 * h + 2, lanes], (8, 128))
                parts.append(jnp.where(first_half, first, second))
            value = value - jnp.concatenate(parts, axis=0) * mult16[c]
        return value

    arrived(dr.at[:, pl.ds(0, PEERS - 1)], d_recv.at[0])
    put(out_r, residual_tile)
    write_r = pltpu.make_async_copy(out_r, res_hbm, l_sem.at[0])
    write_r.start()
    drain()
    arrived(ar.at[:, pl.ds(0, PEERS - 1)], a_recv.at[0])
    put(out_a, lambda t, p: ar[t, p])
    write_a = pltpu.make_async_copy(out_a, adj_hbm, l_sem.at[1])
    write_a.start()

    arrived(as_.at[pl.ds(0, PEERS - 1)], a_send.at[0])
    write_r.wait()
    write_a.wait()


def hand_over(a_in, r_in, a_out, r_out):
    a_out[...] = a_in[...]
    r_out[...] = r_in[...]


def solution(mesh):
    n_span = mesh.shape["span"]
    mats, harm = constants()

    def local(
        adjoint_start,
        source,
        jacobian_tiles,
        tile_columns,
        pseudo_time,
        control_terms,
        surface_rows,
        surface_weight,
        trim_inverse,
    ):
        any_spec = pl.BlockSpec(memory_space=pl.ANY)
        smem = pl.BlockSpec(memory_space=pltpu.SMEM)
        vmem_spec = pl.BlockSpec(memory_space=pltpu.VMEM)
        dma = pltpu.SemaphoreType.DMA
        vm = pltpu.VMEM
        out = jax.ShapeDtypeStruct((OWN, NOBJ, ROWS), F32)
        both = pl.pallas_call(
            lambda *refs: kernel(n_span, *refs),
            out_shape=(out, out),
            in_specs=[smem, smem] + [any_spec] * 9,
            out_specs=(any_spec, any_spec),
            scratch_shapes=[
                vm((NB, OWN, K, TILE, TILE), BF16),
                vm((OWN, NOBJ, ROWS), F32),
                vm((OWN, NOBJ, ROWS), F32),
                vm((3, OWN, ROWS), F32),
                vm((3, 8, 128), F32),
                vm((6, 128), jnp.int32),
                vm((3, S_DEV), F32),
                vm((7, 128, 384), BF16),
                vm((2, 128, 128), F32),
                vm((OWN, NOBJ, ROWS), F32),
                vm((OWN, NOBJ, ROWS), F32),
                vm((3, 8, 32, 128), F32),
                vm((NB + 2, 16, TILE), BF16),
                vm((5, 8, 16, 128), BF16),
                vm((NB + 2, 16, TILE), BF16),
                vm((72, 128), F32),
                vm((3, 8, 16, 128), F32),
                vm((3, 8, 16, 128), F32),
                vm((8, 3, 32, 128), F32),
                vm((8, 3, 16, 128), F32),
                vm((8, 3, 16, 128), F32),
                vm((128, 384), F32),
                vm((128, 384), F32),
                vm((3, 128, 384), F32),
                vm((128, 384), F32),
                vm((8, 3, 16, 128), BF16),
                vm((8, 3, 16, 128), F32),
                vm((3, 8, 16, 128), F32),
                vm((8, 3, 16, 128), F32),
                vm((3, 8, 16, 128), F32),
                vm((2, 1, 128), F32),
                vm((2, n_span, 1, 128), F32),
                vm((2, 1, 128), F32),
                vm((2, PEERS, 1, 128), F32),
                dma((NB,)),
                dma((8,)),
                dma((1,)),
                dma((1,)),
                dma((2,)),
                dma((2,)),
                dma((2,)),
                dma((2,)),
                dma((1,)),
                dma((1,)),
                dma((2,)),
                dma((2,)),
                dma((1,)),
                dma((1,)),
                dma((1,)),
                dma((1,)),
                dma((2,)),
                dma((2,)),
                dma((2,)),
                dma((2,)),
            ],
            compiler_params=pltpu.CompilerParams(
                collective_id=0, has_side_effects=True, vmem_limit_bytes=62 * 1024 * 1024
            ),
        )(
            tile_columns.T,
            trim_inverse,
            adjoint_start,
            source,
            jacobian_tiles,
            pseudo_time.reshape(3, 8, 128),
            control_terms,
            surface_rows.reshape(6, 128),
            surface_weight,
            jnp.asarray(mats),
            jnp.asarray(harm),
        )
        return pl.pallas_call(
            hand_over,
            out_shape=(out, out),
            in_specs=[vmem_spec, vmem_spec],
            out_specs=(vmem_spec, vmem_spec),
        )(*both)

    return jax.shard_map(
        local,
        mesh=mesh,
        in_specs=(
            P("inst", None, "span"),
            P("inst", None, "span"),
            P("inst", "span", None, None, None),
            P("span", None),
            P("span"),
            P(None, "inst", "span"),
            P("span"),
            P(),
            P(),
        ),
        out_specs=(P("inst", None, "span"), P("inst", None, "span")),
        check_vma=False,
    )
```

```python
import math

import jax
import jax.numpy as jnp
import ml_dtypes
import numpy as np
from jax import lax
from jax.experimental import pallas as pl
from jax.experimental.pallas import tpu as pltpu
from jax.sharding import PartitionSpec as P

MESH = pl.DeviceIdType.MESH
F32 = jnp.float32
BF16 = jnp.bfloat16

INST = 32
PEERS = 8
OWN = 4
NOBJ = 4
ROWS = 3072
NB = 12
K = 3
TILE = 256
S_DEV = 768
RATE = 0.25
RELAX = 0.8


def split_const(a):
    hi = a.astype(ml_dtypes.bfloat16)
    lo = (a - hi.astype(np.float64)).astype(ml_dtypes.bfloat16)
    return np.concatenate([hi, hi, lo], axis=-1)


def constants():
    theta = 2.0 * math.pi * np.arange(INST) / INST
    half = INST // 2
    trans = np.concatenate(
        [
            np.cos(np.arange(half + 1)[:, None] * theta[None, :]),
            np.sin(np.arange(1, half)[:, None] * theta[None, :]),
        ]
    )
    spread = theta[:, None] - theta[None, :]
    orders = np.arange(1, half)[:, None, None]
    deriv = -(2.0 / INST) * np.sum(orders * np.sin(orders * spread[None]), axis=0)
    eye = np.eye(NOBJ)
    forward = np.kron(trans, eye)
    back = np.kron(trans.T, eye)
    forward_deriv = RATE * np.kron(trans @ deriv, eye)
    own_deriv = RATE * np.kron(deriv, eye)
    mats = [forward, back, forward_deriv, own_deriv]
    for c in range(3):
        spread_c = np.zeros((128, PEERS, 4, OWN))
        spread_c[:, :, c, :] = np.repeat(trans, NOBJ, axis=0).reshape(128, PEERS, OWN)
        mats.append(spread_c.reshape(128, 128))
    mats = np.stack([split_const(m) for m in mats])
    angle = np.repeat(theta, NOBJ)
    harm = np.stack([np.cos(angle), np.sin(angle)]).astype(np.float32)
    harm = np.ascontiguousarray(np.broadcast_to(harm[:, :, None], (2, 128, 128)))
    return mats, harm


def exact_dot(mat, x):
    hi = x.astype(BF16)
    lo = (x - hi.astype(F32)).astype(BF16)
    return jnp.dot(mat, jnp.concatenate([hi, lo, hi], axis=0), preferred_element_type=F32)


def kernel(
    n_span,
    cols_ref,
    tinv_ref,
    state_hbm,
    source_hbm,
    jac_hbm,
    pt_hbm,
    ct_hbm,
    rows_hbm,
    sw_hbm,
    mats_hbm,
    harm_hbm,
    adj_hbm,
    res_hbm,
    jbuf,
    st_v,
    src_v,
    ct_v,
    pt_v,
    rows_v,
    sw_v,
    mats_v,
    harm_v,
    out_a,
    out_r,
    s0,
    n0,
    n1,
    nf,
    w_v,
    base1,
    base2,
    xs,
    xb1,
    xb2,
    scal,
    yd,
    ctf,
    st1,
    ns,
    ds_,
    dr,
    as_,
    ar,
    r1s,
    r1r,
    r2s,
    r2r,
    j_sem,
    l_sem,
    st_send,
    st_recv,
    h0_send,
    h0_recv,
    b_send,
    b_recv,
    n_send,
    n_recv,
    h1_send,
    h1_recv,
    d_send,
    d_recv,
    a_send,
    a_recv,
    r1_send,
    r1_recv,
    r2_send,
    r2_recv,
):
    me = lax.axis_index("inst")
    sp = lax.axis_index("span")
    last = n_span - 1

    local_in = [
        (state_hbm, st_v),
        (rows_hbm, rows_v),
        (sw_hbm.at[:, pl.ds(pl.multiple_of(sp * S_DEV, S_DEV), S_DEV)], sw_v),
        (harm_hbm, harm_v),
        (ct_hbm, ct_v),
        (source_hbm, src_v),
        (pt_hbm, pt_v),
        (mats_hbm, mats_v),
    ]
    loads = [pltpu.make_async_copy(a, b, l_sem.at[n]) for n, (a, b) in enumerate(local_in)]
    for c in loads:
        c.start()

    def jac_copy(b):
        return pltpu.make_async_copy(jac_hbm.at[:, b], jbuf.at[b], j_sem.at[b])

    @pl.loop(0, NB)
    def _(b):
        jac_copy(b).start()

    zero2 = jnp.zeros((2, 16, 128), BF16)
    n1[0, 6:8] = zero2
    n1[4, 0:2] = zero2
    for column in (0, NB + 1):
        n0[column] = jnp.zeros((16, TILE), BF16)

    barrier = pltpu.get_barrier_semaphore()

    def signal(i, s):
        pl.semaphore_signal(barrier, inc=1, device_id=(i, s), device_id_type=MESH)

    def peers(fn):
        for d in (5, 4, 7, 6, 3, 2, 1):
            fn(jnp.bitwise_xor(me, d))

    def far_first(fn):
        for d in (5, 4, 7, 6, 3, 2, 1):
            fn(jnp.bitwise_xor(me, d))

    def spans(fn):
        for d in range(1, n_span):
            fn(lax.rem(sp + d, n_span))

    peers(lambda p: signal(p, sp))
    spans(lambda q: signal(me, q))

    has_low = sp > 0
    has_high = sp < last
    def at_low(fn):
        @pl.when(has_low)
        def _():
            @pl.when(me < 2)
            def _():
                pl.loop(0, PEERS)(fn)

    def at_high(fn):
        @pl.when(has_high)
        def _():
            @pl.when(me >= PEERS - 2)
            def _():
                pl.loop(0, PEERS)(fn)

    def around(p):
        signal(p, lax.rem(sp + 1, n_span))
        signal(p, lax.rem(sp + n_span - 1, n_span))

    peers(around)

    loads[0].wait()
    flat = jnp.concatenate([st_v[i] for i in range(OWN)], axis=0)
    for q in range(24):
        piece = flat[:, q * 128 : (q + 1) * 128]
        s0[q // 8, q % 8, 0:16] = piece
    loads[4].wait()
    flat_c = jnp.concatenate([ct_v[c] for c in range(3)] + [jnp.zeros((OWN, ROWS), F32)], axis=0)
    for q in range(24):
        s0[q // 8, q % 8, 16:32] = flat_c[:, q * 128 : (q + 1) * 128]
    for b in range(NB):
        n0[b + 1] = flat[:, b * TILE : (b + 1) * TILE].astype(BF16)

    pl.semaphore_wait(barrier, 3 * (PEERS - 1) + n_span - 1)

    def to(src, dst, send, recv, i, s):
        return pltpu.make_async_remote_copy(
            src_ref=src, dst_ref=dst, send_sem=send, recv_sem=recv, device_id=(i, s), device_id_type=MESH
        )

    def halo0_low():
        return to(n0.at[1], n0.at[NB + 1], h0_send.at[0], h0_recv.at[0], me, sp - 1)

    def halo0_high():
        return to(n0.at[NB], n0.at[0], h0_send.at[1], h0_recv.at[1], me, sp + 1)

    def state_out(p):
        return to(s0.at[:, p], xs.at[me], st_send.at[0], st_recv.at[0], p, sp)

    def base_out(k, t, p):
        src, dst = (base1, xb1) if k == 0 else (base2, xb2)
        return to(src.at[t, p], dst.at[me, t], b_send.at[k], b_recv.at[k], p, sp)

    def narrow_out(p):
        return to(ns.at[p], n1.at[pl.ds(1, 3), me], n_send.at[0], n_recv.at[0], p, sp)

    def halo1_low(p):
        return to(ns.at[p, 0], n1.at[4, me], h1_send.at[0], h1_recv.at[0], p, sp - 1)

    def halo1_high(p):
        return to(ns.at[p, 2], n1.at[0, me], h1_send.at[1], h1_recv.at[1], p, sp + 1)

    def deriv_out(p):
        return to(ds_.at[p], dr.at[:, me], d_send.at[0], d_recv.at[0], p, sp)

    def adj_out(p):
        return to(as_.at[p], ar.at[:, me], a_send.at[0], a_recv.at[0], p, sp)

    def sum1_out(k, q):
        return to(r1s.at[k], r1r.at[k, sp], r1_send.at[k], r1_recv.at[k], me, q)

    def sum2_out(k, p):
        return to(r2s.at[k], r2r.at[k, me], r2_send.at[k], r2_recv.at[k], p, sp)

    def arrived(dst, sem):
        pltpu.make_async_copy(dst, dst, sem).wait()

    @pl.when(has_low)
    def _():
        halo0_low().start()

    @pl.when(has_high)
    def _():
        halo0_high().start()

    loads[1].wait()
    loads[2].wait()
    rows = jnp.concatenate([rows_v[q : q + 1, :] for q in range(6)], axis=1)
    high, low = lax.div(rows, 128), lax.rem(rows, 128)
    tiles24 = lax.broadcasted_iota(jnp.int32, (24, S_DEV), 0)
    hit = jnp.broadcast_to(high, (24, S_DEV)) == tiles24
    spread = jnp.concatenate(
        [jnp.where(hit, jnp.broadcast_to(sw_v[c : c + 1, :], (24, S_DEV)), 0.0) for c in range(3)], axis=0
    )
    spread_hi = spread.astype(BF16)
    spread_lo = (spread - spread_hi.astype(F32)).astype(BF16)
    lane_hit = jnp.broadcast_to(low, (128, S_DEV)) == lax.broadcasted_iota(jnp.int32, (128, S_DEV), 0)
    lane_hit = jnp.where(lane_hit, 1.0, 0.0).astype(BF16)
    nt = (((1,), (1,)), ((), ()))
    w_v[...] = lax.dot_general(spread_hi, lane_hit, nt, preferred_element_type=F32) + lax.dot_general(
        spread_lo, lane_hit, nt, preferred_element_type=F32
    )

    lane8 = lax.broadcasted_iota(jnp.int32, (8, 128), 1)
    row8 = lax.rem(lax.broadcasted_iota(jnp.int32, (8, 128), 0), NOBJ)

    def load_row(accs):
        total = jnp.zeros((8, 128), F32)
        for c in range(3):
            col = jnp.sum(accs[c], axis=1, keepdims=True)
            total = total + jnp.where(lane8 == c * NOBJ + row8, jnp.broadcast_to(col, (8, 128)), 0.0)
        return jnp.sum(total, axis=0, keepdims=True)

    loads[3].wait()
    accs = []
    for c in range(3):
        acc = jnp.zeros((16, 128), F32)
        for q in range(24):
            acc = acc + s0[q // 8, q % 8, 0:16] * jnp.broadcast_to(w_v[c * 24 + q : c * 24 + q + 1, :], (16, 128))
        if c > 0:
            acc = acc * harm_v[c - 1, pl.ds(pl.multiple_of(me * 16, 16), 16), :]
        accs.append(acc[0:8] + acc[8:16])

    def start_sum(k, row):
        r1s[k] = row
        r1r[k, pl.ds(sp, 1)] = row.reshape(1, 1, 128)
        spans(lambda q: sum1_out(k, q).start())

    start_sum(0, load_row(accs))
    far_first(lambda p: state_out(p).start())
    xs[pl.ds(me, 1)] = s0[:, pl.ds(me, 1)].reshape(1, 3, 32, 128)

    def middle_sum(k):
        arrived(r1r.at[k, pl.ds(0, n_span - 1)], r1_recv.at[k])
        row = jnp.sum(r1r[k], axis=0)
        r2s[k] = row
        r2r[k, pl.ds(me, 1)] = row.reshape(1, 1, 128)
        far_first(lambda p: sum2_out(k, p).start())

    def multiplier(k):
        arrived(r2r.at[k, pl.ds(0, PEERS - 1)], r2_recv.at[k])
        row = jnp.broadcast_to(jnp.sum(r2r[k], axis=0), (8, 128))
        out = []
        for c in range(3):
            mask = jnp.zeros((8, 128), F32)
            for d in range(3):
                mask = jnp.where(lane8 == d * NOBJ + row8, tinv_ref[c, d], mask)
            col = jnp.sum(row * mask, axis=1, keepdims=True)
            out.append(jnp.broadcast_to(col, (8, 128)))
        return out

    inst_row = lax.div(lax.broadcasted_iota(jnp.int32, (16, TILE), 0), NOBJ)
    masks = [jnp.where(inst_row == i, 1.0, 0.0).astype(BF16) for i in range(OWN)]

    def product(b, narrow, base):
        blocks = [narrow[cols_ref[k, b] + 1] for k in range(K)]
        left = jnp.concatenate([blocks[k] * masks[i] for i in range(OWN) for k in range(K)], axis=1)
        acc = jnp.dot(left, jbuf[b].reshape(OWN * K * TILE, TILE), preferred_element_type=F32)
        rows = jnp.concatenate([src_v[i, :, b * TILE : (b + 1) * TILE] for i in range(OWN)], axis=0)
        value = rows - acc
        for half in range(2):
            q = 2 * b + half
            base[q // 8, q % 8] = value[:, half * 128 : (half + 1) * 128]

    def sweep_products(k, narrow, base, landed):
        for t in range(3):
            for b in range(4 * t, 4 * t + 4):
                if k == 0:
                    jac_copy(b).wait()
                product(b, narrow, base)
            far_first(lambda p: base_out(k, t, p).start())
            landed[pl.ds(me, 1), t] = base[t, pl.ds(me, 1)]
            if t == 2 - k:
                middle_sum(k)

    def wide(ref):
        return jnp.concatenate([ref[:, t].reshape(128, 128) for t in range(3)], axis=1)

    def wide_part(ref, first):
        parts = [ref[:, t, first : first + 16].reshape(128, 128) for t in range(3)]
        return jnp.concatenate(parts, axis=1)

    def add_control(k):
        mult = multiplier(k)
        total = yd[...].reshape(16, 8, 384)
        for c in range(3):
            total = total - ctf[c].reshape(16, 8, 384) * jnp.concatenate([mult[c]] * 3, axis=1)[None]
        yd[...] = total.reshape(128, 384)
        return mult

    @pl.when(has_high)
    def _():
        arrived(n0.at[NB + 1], h0_recv.at[0])

    @pl.when(has_low)
    def _():
        arrived(n0.at[0], h0_recv.at[1])

    loads[5].wait()
    sweep_products(0, n0, base1, xb1)

    for c in loads[6:]:
        c.wait()
    order = lax.div(lax.broadcasted_iota(jnp.int32, (128, 128), 0), NOBJ)
    freq = jnp.where(order > INST // 2, order - INST // 2, order)
    ends = jnp.logical_or(freq == 0, freq == INST // 2)
    weight = jnp.where(ends, RELAX / INST, 2.0 * RELAX / INST)
    offset = RATE * freq.astype(F32)
    for t in range(3):
        pt = jnp.broadcast_to(pt_v[t, pl.ds(me, 1), :], (128, 128))
        scal[:, t * 128 : (t + 1) * 128] = weight / (pt + offset)
    arrived(xs.at[pl.ds(0, PEERS - 1)], st_recv.at[0])
    state0 = wide_part(xs, 0)
    yd[...] = exact_dot(mats_v[2], state0)
    control = wide_part(xs, 16)
    for c in range(3):
        ctf[c] = exact_dot(mats_v[4 + c], control)
    add_control(0)

    def wait_base(k):
        arrived((xb1 if k == 0 else xb2).at[pl.ds(0, PEERS - 1)], b_recv.at[k])

    wait_base(0)
    spectrum = exact_dot(mats_v[0], wide(xb1)) + yd[...]
    state1 = wide_part(xs, 0) + exact_dot(mats_v[1], spectrum * scal[...])
    st1[...] = state1
    for t in range(3):
        piece = state1[:, t * 128 : (t + 1) * 128]
        ns[:, t] = piece.astype(BF16).reshape(PEERS, 16, 128)
    far_first(lambda p: narrow_out(p).start())

    at_low(lambda p: halo1_low(p).start())
    at_high(lambda p: halo1_high(p).start())

    n1[pl.ds(1, 3), pl.ds(me, 1)] = ns[pl.ds(me, 1)].reshape(3, 1, 16, 128)

    accs = []
    for c in range(3):
        acc = jnp.zeros((128, 128), F32)
        for t in range(3):
            weight = w_v[pl.ds(c * 24 + t * 8 + me, 1), :]
            acc = acc + state1[:, t * 128 : (t + 1) * 128] * jnp.broadcast_to(weight, (128, 128))
        if c > 0:
            acc = acc * harm_v[c - 1]
        accs.append(jnp.sum(acc.reshape(16, 8, 128), axis=0))
    start_sum(1, load_row(accs))

    yd[...] = exact_dot(mats_v[2], state1)
    arrived(n1.at[pl.ds(1, 3), pl.ds(0, PEERS - 1)], n_recv.at[0])

    @pl.when(has_high)
    def _():
        arrived(n1.at[4, pl.ds(0, 2)], h1_recv.at[0])

    @pl.when(has_low)
    def _():
        arrived(n1.at[0, pl.ds(PEERS - 2, 2)], h1_recv.at[1])

    for column in range(NB + 2):
        slot = 2 * column + 6
        left, right = n1[slot // 8, slot % 8], n1[slot // 8, slot % 8 + 1]
        nf[column] = jnp.concatenate([left, right], axis=1)

    sweep_products(1, nf, base2, xb2)
    derived = exact_dot(mats_v[3], st1[...])
    for t in range(3):
        ds_[:, t] = derived[:, t * 128 : (t + 1) * 128].reshape(PEERS, 16, 128)
    far_first(lambda p: deriv_out(p).start())
    dr[:, pl.ds(me, 1)] = ds_[pl.ds(me, 1)].reshape(3, 1, 16, 128)

    mult = add_control(1)

    wait_base(1)
    spectrum = exact_dot(mats_v[0], wide(xb2)) + yd[...]
    final = st1[...] + exact_dot(mats_v[1], spectrum * scal[...])
    for t in range(3):
        as_[:, t] = final[:, t * 128 : (t + 1) * 128].reshape(PEERS, 16, 128)
    far_first(lambda p: adj_out(p).start())
    ar[:, pl.ds(me, 1)] = as_[pl.ds(me, 1)].reshape(3, 1, 16, 128)

    def drain():
        @pl.when(has_low)
        def _():
            halo0_low().wait_send()

        @pl.when(has_high)
        def _():
            halo0_high().wait_send()

        @pl.when(has_low)
        def _():
            @pl.when(me < 2)
            def _():
                arrived(ns.at[:, 0], h1_send.at[0])

        @pl.when(has_high)
        def _():
            @pl.when(me >= PEERS - 2)
            def _():
                arrived(ns.at[:, 2], h1_send.at[1])

        arrived(s0.at[:, pl.ds(0, PEERS - 1)], st_send.at[0])
        arrived(ns.at[pl.ds(0, PEERS - 1)], n_send.at[0])
        arrived(ds_.at[pl.ds(0, PEERS - 1)], d_send.at[0])
        for k, base in ((0, base1), (1, base2)):
            arrived(base.at[:, pl.ds(0, PEERS - 1)], b_send.at[k])
            arrived(r1r.at[k, pl.ds(0, n_span - 1)], r1_send.at[k])
            arrived(r2r.at[k, pl.ds(0, PEERS - 1)], r2_send.at[k])

    def put(out, fn):
        for q in range(24):
            value = fn(q // 8, q % 8)
            for i in range(OWN):
                out[i, :, q * 128 : (q + 1) * 128] = value[i * NOBJ : (i + 1) * NOBJ, :]

    mult16 = [jnp.concatenate([m, m], axis=0) for m in mult]
    first_half = lax.div(lax.broadcasted_iota(jnp.int32, (8, 128), 0), NOBJ) == 0

    def residual_tile(t, p):
        q = t * 8 + p
        lanes = slice(q * 128, (q + 1) * 128)
        value = base2[t, p] + dr[t, p]
        for c in range(3):
            parts = []
            for h in range(2):
                first = jnp.broadcast_to(ct_v[c, 2 * h : 2 * h + 1, lanes], (8, 128))
                second = jnp.broadcast_to(ct_v[c, 2 * h + 1 : 2 * h + 2, lanes], (8, 128))
                parts.append(jnp.where(first_half, first, second))
            value = value - jnp.concatenate(parts, axis=0) * mult16[c]
        return value

    arrived(dr.at[:, pl.ds(0, PEERS - 1)], d_recv.at[0])
    put(out_r, residual_tile)
    write_r = pltpu.make_async_copy(out_r, res_hbm, l_sem.at[0])
    write_r.start()
    drain()
    arrived(ar.at[:, pl.ds(0, PEERS - 1)], a_recv.at[0])
    put(out_a, lambda t, p: ar[t, p])
    write_a = pltpu.make_async_copy(out_a, adj_hbm, l_sem.at[1])
    write_a.start()

    arrived(as_.at[pl.ds(0, PEERS - 1)], a_send.at[0])
    write_r.wait()
    write_a.wait()


def hand_over(a_in, r_in, a_out, r_out):
    a_out[...] = a_in[...]
    r_out[...] = r_in[...]


def solution(mesh):
    n_span = mesh.shape["span"]
    mats, harm = constants()

    def local(
        adjoint_start,
        source,
        jacobian_tiles,
        tile_columns,
        pseudo_time,
        control_terms,
        surface_rows,
        surface_weight,
        trim_inverse,
    ):
        any_spec = pl.BlockSpec(memory_space=pl.ANY)
        smem = pl.BlockSpec(memory_space=pltpu.SMEM)
        vmem_spec = pl.BlockSpec(memory_space=pltpu.VMEM)
        dma = pltpu.SemaphoreType.DMA
        vm = pltpu.VMEM
        out = jax.ShapeDtypeStruct((OWN, NOBJ, ROWS), F32)
        both = pl.pallas_call(
            lambda *refs: kernel(n_span, *refs),
            out_shape=(out, out),
            in_specs=[smem, smem] + [any_spec] * 9,
            out_specs=(any_spec, any_spec),
            scratch_shapes=[
                vm((NB, OWN, K, TILE, TILE), BF16),
                vm((OWN, NOBJ, ROWS), F32),
                vm((OWN, NOBJ, ROWS), F32),
                vm((3, OWN, ROWS), F32),
                vm((3, 8, 128), F32),
                vm((6, 128), jnp.int32),
                vm((3, S_DEV), F32),
                vm((7, 128, 384), BF16),
                vm((2, 128, 128), F32),
                vm((OWN, NOBJ, ROWS), F32),
                vm((OWN, NOBJ, ROWS), F32),
                vm((3, 8, 32, 128), F32),
                vm((NB + 2, 16, TILE), BF16),
                vm((5, 8, 16, 128), BF16),
                vm((NB + 2, 16, TILE), BF16),
                vm((72, 128), F32),
                vm((3, 8, 16, 128), F32),
                vm((3, 8, 16, 128), F32),
                vm((8, 3, 32, 128), F32),
                vm((8, 3, 16, 128), F32),
                vm((8, 3, 16, 128), F32),
                vm((128, 384), F32),
                vm((128, 384), F32),
                vm((3, 128, 384), F32),
                vm((128, 384), F32),
                vm((8, 3, 16, 128), BF16),
                vm((8, 3, 16, 128), F32),
                vm((3, 8, 16, 128), F32),
                vm((8, 3, 16, 128), F32),
                vm((3, 8, 16, 128), F32),
                vm((2, 1, 128), F32),
                vm((2, n_span, 1, 128), F32),
                vm((2, 1, 128), F32),
                vm((2, PEERS, 1, 128), F32),
                dma((NB,)),
                dma((8,)),
                dma((1,)),
                dma((1,)),
                dma((2,)),
                dma((2,)),
                dma((2,)),
                dma((2,)),
                dma((1,)),
                dma((1,)),
                dma((2,)),
                dma((2,)),
                dma((1,)),
                dma((1,)),
                dma((1,)),
                dma((1,)),
                dma((2,)),
                dma((2,)),
                dma((2,)),
                dma((2,)),
            ],
            compiler_params=pltpu.CompilerParams(
                collective_id=0, has_side_effects=True, vmem_limit_bytes=62 * 1024 * 1024
            ),
        )(
            tile_columns.T,
            trim_inverse,
            adjoint_start,
            source,
            jacobian_tiles,
            pseudo_time.reshape(3, 8, 128),
            control_terms,
            surface_rows.reshape(6, 128),
            surface_weight,
            jnp.asarray(mats),
            jnp.asarray(harm),
        )
        return pl.pallas_call(
            hand_over,
            out_shape=(out, out),
            in_specs=[vmem_spec, vmem_spec],
            out_specs=(vmem_spec, vmem_spec),
        )(*both)

    return jax.shard_map(
        local,
        mesh=mesh,
        in_specs=(
            P("inst", None, "span"),
            P("inst", None, "span"),
            P("inst", "span", None, None, None),
            P("span", None),
            P("span"),
            P(None, "inst", "span"),
            P("span"),
            P(),
            P(),
        ),
        out_specs=(P("inst", None, "span"), P("inst", None, "span")),
        check_vma=False,
    )
```
